32 devices in a mesh: dp: 4 (over x, core), blk: 2 (over y), ulysses: 4 (over z).
Axes of the slice: x: 2, y: 2, z: 4, core: 2. Of those that a mesh axis runs over, the one named last changes fastest.
Arguments:
- hidden: bfloat16 [8, 2048, 1024], P('dp', ('blk', 'ulysses')), may hold values from -6 to 6
- positions: int32 [8, 2048], P('dp', 'blk'), may hold values from 0 to 2047, as said below
- ln1_gain: bfloat16 [1024], P(('dp', 'blk', 'ulysses')), may hold values from 0.5 to 1.5
- ln1_bias: bfloat16 [1024], P(('dp', 'blk', 'ulysses')), may hold values from -2 to 2
- ln2_gain: bfloat16 [1024], P(('dp', 'blk', 'ulysses')), may hold values from 0.5 to 1.5
- ln2_bias: bfloat16 [1024], P(('dp', 'blk', 'ulysses')), may hold values from -2 to 2
- qkv_weight: bfloat16 [1024, 3072], P(('dp', 'blk', 'ulysses')), may hold values from -0.25 to 0.25
- qkv_bias: bfloat16 [3072], P(('dp', 'blk', 'ulysses')), may hold values from -2 to 2
- dense_weight: bfloat16 [1024, 1024], P(('dp', 'blk', 'ulysses')), may hold values from -1.5 to 1.5
- dense_bias: bfloat16 [1024], P(('dp', 'blk', 'ulysses')), may hold values from -2 to 2
- up_weight: bfloat16 [1024, 4096], P(('dp', 'blk', 'ulysses')), may hold values from -0.1875 to 0.1875
- up_bias: bfloat16 [4096], P(('dp', 'blk', 'ulysses')), may hold values from -2 to 2
- down_weight: bfloat16 [4096, 1024], P(('dp', 'blk', 'ulysses')), may hold values from -0.09375 to 0.09375
- down_bias: bfloat16 [1024], P(('dp', 'blk', 'ulysses')), may hold values from -2 to 2
- cotangent: bfloat16 [8, 2048, 1024], P('dp', ('blk', 'ulysses')), may hold values from -6 to 6
Outputs:
- output: bfloat16 [8, 2048, 1024], P('dp', ('blk', 'ulysses'))
- input_grad: bfloat16 [8, 2048, 1024], P('dp', ('blk', 'ulysses'))
- ln1_gain_grad: float32 [1024], P(('dp', 'blk', 'ulysses'))
- ln1_bias_grad: float32 [1024], P(('dp', 'blk', 'ulysses'))
- ln2_gain_grad: float32 [1024], P(('dp', 'blk', 'ulysses'))
- ln2_bias_grad: float32 [1024], P(('dp', 'blk', 'ulysses'))
- qkv_weight_grad: float32 [1024, 3072], P(('dp', 'blk', 'ulysses'))
- qkv_bias_grad: float32 [3072], P(('dp', 'blk', 'ulysses'))
- dense_weight_grad: float32 [1024, 1024], P(('dp', 'blk', 'ulysses'))
- dense_bias_grad: float32 [1024], P(('dp', 'blk', 'ulysses'))
- up_weight_grad: float32 [1024, 4096], P(('dp', 'blk', 'ulysses'))
- up_bias_grad: float32 [4096], P(('dp', 'blk', 'ulysses'))
- down_weight_grad: float32 [4096, 1024], P(('dp', 'blk', 'ulysses'))
- down_bias_grad: float32 [1024], P(('dp', 'blk', 'ulysses'))
The draws below stay inside these ranges and needn't reach their ends.
Inputs may be any that keep to these rules, and one draw needn't show every extreme that they name: positions restart at 0 at each document's first token and rise by one along it; in each group of 2 sequences of one index of dp, one whole sequence is a single document.
All inputs are finite; a program needn't handle non-finite values.
Results may differ from the reference program's by a relative error of at most 0.012.
The reference program's roundings to bfloat16 on the way count: a program that leaves them out, or rounds other values in their place, can miss the bound.
Values may be sent and summed in bfloat16 or wider, within the bound.
No kernel may reach another device: no remote copies, remote signals or barrier semaphores. Data moves between devices by JAX's collectives and lax.ppermute only.
A program may use at most 192 MiB of HBM per device.

```python
import jax
import jax.numpy as jnp
from jax import lax

D = 1024
HEADS = 16
HEAD_DIM = 64
ROT = 16
FF = 4096
SEQ_DP = 2
LEN = 2048
SEQS = 8


def draw_positions(key, part):
    key = jax.random.fold_in(key, 11)
    first, second = jax.random.split(key)
    index = jnp.arange(LEN, dtype=jnp.int32)
    cuts = jax.random.randint(first, (SEQS, LEN), 0, max(LEN // 4, 2)) == 0
    chosen = jax.random.randint(second, (SEQS // SEQ_DP,), 0, SEQ_DP)
    whole = jnp.arange(SEQS, dtype=jnp.int32) % SEQ_DP == jnp.repeat(chosen, SEQ_DP)
    cuts = cuts & jnp.logical_not(whole[:, None]) | (index[None, :] == 0)
    begins = jnp.where(cuts, index[None, :], 0)
    return index[None, :] - lax.cummax(begins, axis=1)


def shard_levels(rng, dims, shards, smallest, largest):
    def one(axis_at, shards_of):
        steps = jax.random.uniform(jax.random.fold_in(jax.random.fold_in(rng, 6), axis_at), (shards_of,), jnp.float32, smallest / len(shards), largest / len(shards))
        return jnp.repeat(jnp.exp(steps), dims[axis_at] // shards_of).reshape((-1,) + (1,) * (len(dims) - axis_at - 1))

    level = one(*shards[0])
    for cut in shards[1:]:
        level = level * one(*cut)
    return level


def bell_draw(key, dims, scale, limit, pieces=(), kind=jnp.bfloat16):
    result = jax.random.normal(key, dims, jnp.float32) * scale
    if len(pieces) > 0:
        result = shard_levels(key, dims, pieces, -0.22, 0.18) * result
    return jnp.clip(result, min=-limit, max=limit).astype(kind)


def setup_inputs(seed: int = 0) -> dict:
    arg_keys = jax.random.split(jax.random.key(seed), 16)
    return {
        "hidden": bell_draw(arg_keys[0], (SEQS, LEN, D), 1.0, 6.0, ((0, 4), (1, 8))),
        "positions": draw_positions(jax.random.fold_in(arg_keys[15], 71), 0),
        "ln1_gain": jnp.clip(1.0 + 0.1 * jax.random.normal(arg_keys[2], (D,), jnp.float32), 0.5, 1.5).astype(jnp.bfloat16),
        "ln1_bias": bell_draw(arg_keys[3], (D,), 0.3, 2.0, ((0, 32),)),
        "ln2_gain": jnp.clip(1.0 + 0.1 * jax.random.normal(arg_keys[4], (D,), jnp.float32), 0.5, 1.5).astype(jnp.bfloat16),
        "ln2_bias": bell_draw(arg_keys[5], (D,), 0.3, 2.0, ((0, 32),)),
        "qkv_weight": bell_draw(arg_keys[6], (D, 3 * D), (D // 2) ** -0.5, 0.25, ((0, 32),)),
        "qkv_bias": bell_draw(arg_keys[7], (3 * D,), 0.3, 2.0, ((0, 32),)),
        "dense_weight": bell_draw(arg_keys[8], (D, D), (D // 64) ** -0.5, 1.5, ((0, 32),)),
        "dense_bias": bell_draw(arg_keys[9], (D,), 0.3, 2.0, ((0, 32),)),
        "up_weight": bell_draw(arg_keys[10], (D, FF), D ** -0.5, 0.1875, ((0, 32),)),
        "up_bias": bell_draw(arg_keys[11], (FF,), 0.3, 2.0, ((0, 32),)),
        "down_weight": bell_draw(arg_keys[12], (FF, D), FF ** -0.5, 0.09375, ((0, 32),)),
        "down_bias": bell_draw(arg_keys[13], (D,), 0.3, 2.0, ((0, 32),)),
        "cotangent": bell_draw(arg_keys[14], (SEQS, LEN, D), 1.0, 6.0, ((0, 4), (1, 8))),
    }


FULL_PRECISION = lax.Precision.HIGHEST
EPSILON = 1e-05
MASKED_SCORE = -1e+30

@jax.custom_vjp
def low(v):
    return lax.optimization_barrier(v.astype(jnp.bfloat16)).astype(jnp.float32)

@jax.custom_vjp
def low_back(v):
    return v

def low_keep(v):
    return (low(v), None)

def low_pass(kept, grad):
    return (grad,)

def back_keep(v):
    return (v, None)

def back_low(kept, grad):
    return (low(grad),)
low.defvjp(low_keep, low_pass)
low_back.defvjp(back_keep, back_low)

def layer_norm(value_rows, gain, shift):
    center = value_rows - lax.optimization_barrier(jnp.mean(value_rows, axis=-1, keepdims=True))
    spread = lax.optimization_barrier(jnp.mean(center * center, axis=-1, keepdims=True))
    return center * lax.rsqrt(spread + EPSILON) * gain + shift

def frequencies():
    return 10000.0 ** (-(jnp.arange(ROT // 2, dtype=jnp.float32) * 2.0 / ROT))

def rope_pair(joined, angles):
    half = ROT // 2
    cosine = jnp.cos(angles)[:, :, None, None, :]
    sine = jnp.sin(angles)[:, :, None, None, :]
    former = joined[..., :half]
    latter = joined[..., half:ROT]
    turned = jnp.concatenate([former * cosine - latter * sine, latter * cosine + former * sine, joined[..., ROT:]], axis=-1)
    rotated = (jnp.arange(3, dtype=jnp.int32) < 2)[None, None, :, None, None]
    return jnp.where(rotated, turned, joined)

def project(value_rows, weight_matrix):
    return jnp.einsum('qti,iw->qtw', value_rows, weight_matrix, precision=FULL_PRECISION)

def attend_one(inputs_one):
    query, keyed, valued, starts = inputs_one
    row_count = min(512, LEN)
    block_count = LEN // row_count
    key_index = jnp.arange(LEN, dtype=jnp.int32)
    score_scale = HEAD_DIM ** (-0.5)

    @jax.checkpoint
    def query_block(index):
        query_rows = lax.dynamic_slice_in_dim(query, index * row_count, row_count, 0)
        start_rows = lax.dynamic_slice_in_dim(starts, index * row_count, row_count, 0)
        query_index = index * row_count + jnp.arange(row_count, dtype=jnp.int32)
        score_matrix = low_back(jnp.einsum('qhd,khd->hqk', query_rows, keyed, precision=FULL_PRECISION) * score_scale)
        key_mask = (key_index[None, :] <= query_index[:, None]) & (key_index[None, :] >= start_rows[:, None])
        score_matrix = jnp.where(key_mask[None], score_matrix, MASKED_SCORE)
        probability = jax.nn.softmax(score_matrix, axis=-1)
        return jnp.einsum('hqk,khd->qhd', low(probability), valued, precision=FULL_PRECISION)
    attended = lax.map(query_block, jnp.arange(block_count, dtype=jnp.int32))
    return attended.reshape(LEN, HEADS, HEAD_DIM)

def layer(inputs, ln1_gain, ln1_bias, ln2_gain, ln2_bias, qkv_weight, qkv_bias, dense_weight, dense_bias, up_weight, up_bias, down_weight, down_bias, positions):
    norm1 = low(layer_norm(inputs, ln1_gain, ln1_bias))
    norm2 = low(layer_norm(inputs, ln2_gain, ln2_bias))
    joined = low_back(project(norm1, qkv_weight) + qkv_bias)
    joined = joined.reshape(SEQS, LEN, 3, HEADS, HEAD_DIM)
    angles = positions.astype(jnp.float32)[..., None] * frequencies()
    turned = low(low_back(rope_pair(joined, angles)))
    starts = jnp.arange(LEN, dtype=jnp.int32)[None, :] - positions
    attended = lax.map(attend_one, (turned[:, :, 0], turned[:, :, 1], turned[:, :, 2], starts))
    mixed = low(low_back(attended.reshape(SEQS, LEN, HEADS * HEAD_DIM)))
    branch_attn = project(mixed, dense_weight) + dense_bias
    up_pre = low_back(project(norm2, up_weight) + up_bias)
    active = low(jax.nn.gelu(up_pre, approximate=False))
    branch_mlp = project(active, down_weight) + down_bias
    return inputs + branch_attn + branch_mlp

def reference(hidden, positions, ln1_gain, ln1_bias, ln2_gain, ln2_bias, qkv_weight, qkv_bias, dense_weight, dense_bias, up_weight, up_bias, down_weight, down_bias, cotangent):
    params = (ln1_gain, ln1_bias, ln2_gain, ln2_bias, qkv_weight, qkv_bias, dense_weight, dense_bias, up_weight, up_bias, down_weight, down_bias)
    params = tuple((value.astype(jnp.float32) for value in params))

    def closed(*value_rows):
        return layer(*value_rows, positions)
    final_output, pullback = jax.vjp(closed, hidden.astype(jnp.float32), *params)
    grads = pullback(cotangent.astype(jnp.float32))
    return (final_output.astype(jnp.bfloat16), grads[0].astype(jnp.bfloat16), grads[1], grads[2], grads[3], grads[4], grads[5], grads[6], grads[7], grads[8], grads[9], grads[10], grads[11], grads[12])
```

```python
from functools import partial

import jax
import jax.numpy as jnp
from jax import lax
from jax.experimental import pallas as pl
from jax.experimental.pallas import tpu as pltpu
from jax.sharding import PartitionSpec as P

HEADS = 16
HEAD_DIM = 64
ROT = 16
EPSILON = 1e-05
MASKED_SCORE = -1e30
LOG2_E = 1.4426950408889634
RANKS = ("blk", "ulysses")
F32 = jnp.float32
BF16 = jnp.bfloat16
NN = (((1,), (0,)), ((), ()))
NT = (((1,), (1,)), ((), ()))
TN = (((0,), (0,)), ((), ()))
ANY = pl.BlockSpec(memory_space=pl.ANY)
VMEM = pl.BlockSpec(memory_space=pltpu.VMEM)
SMEM = pl.BlockSpec(memory_space=pltpu.SMEM)


def dot(left, right, dims=NN):
    return lax.dot_general(left, right, dims, preferred_element_type=F32)


def swap(value, axis, bit):
    size = lax.axis_size(axis)
    return lax.ppermute(value, axis, [(i, i ^ bit) for i in range(size)])


def bits_of(size):
    return [1 << k for k in range(size.bit_length() - 1)]


def gather(value, stages):
    for axis, bit in stages:
        value = jnp.concatenate([value, swap(value, axis, bit)], axis=0)
    return value


def natural_weight(axis, bit):
    ulysses = lax.axis_size("ulysses")
    if axis == "ulysses":
        return bit
    if axis == "blk":
        return bit * ulysses
    return (bit // 2) * ulysses * lax.axis_size("blk")


def slots_of(stages, mine):
    relative = jnp.arange(1 << len(stages), dtype=jnp.int32) ^ mine
    slot = jnp.zeros_like(relative)
    for at, (axis, bit) in enumerate(stages):
        slot = slot + (((relative // natural_weight(axis, bit)) % 2) << at)
    return slot


def own_bit(axis, bit):
    return (lax.axis_index(axis) // bit) % 2


def pick(value, index, dim):
    return lax.dynamic_index_in_dim(value, index, dim, keepdims=False)


def reduce_stage(total, dim, axis, bit, wire=BF16):
    mine = own_bit(axis, bit)
    sent = pick(total, 1 - mine, dim).astype(wire)
    return pick(total, mine, dim) + swap(sent, axis, bit).astype(F32)


def params(mib):
    return pltpu.CompilerParams(vmem_limit_bytes=mib << 20)


def place_qkv_kernel(slot_a, slot_b, a_ref, b_ref, qkv_ref, dense_ref):
    rows, width = a_ref.shape[1] // 2, a_ref.shape[2]
    half = width // 2
    for part in range(2):
        span = slice(part * rows, (part + 1) * rows)
        qkv_ref[0, part, 0, :, :width] = a_ref[0, span, :]
        qkv_ref[0, part, 0, :, width:] = b_ref[0, span, :half]
        dense_ref[0, :, part * half : (part + 1) * half] = b_ref[0, span, half:]


def place_qkv(a, b, slot_a, slot_b, planes):
    pieces, rows2, width = a.shape
    rows = rows2 // 2
    inner = pieces // planes
    qkv, dense = pl.pallas_call(
        place_qkv_kernel,
        grid_spec=pltpu.PrefetchScalarGridSpec(
            num_scalar_prefetch=2,
            grid=(pieces,),
            in_specs=[
                pl.BlockSpec((1, rows2, width), lambda p, ta, tb: (ta[p], 0, 0)),
                pl.BlockSpec((1, rows2, width), lambda p, ta, tb: (tb[p], 0, 0)),
            ],
            out_specs=[
                pl.BlockSpec(
                    (1, 2, 1, rows, width + width // 2),
                    lambda p, ta, tb: (p // inner, 0, p % inner, 0, 0),
                ),
                pl.BlockSpec((1, rows, width), lambda p, ta, tb: (p, 0, 0)),
            ],
        ),
        out_shape=[
            jax.ShapeDtypeStruct((planes, 2, inner, rows, width + width // 2), a.dtype),
            jax.ShapeDtypeStruct((pieces, rows, width), a.dtype),
        ],
        name="place_qkv",
    )(slot_a, slot_b, a, b)
    return qkv.reshape(pieces * rows2, -1), dense.reshape(pieces * rows, width)


def place_up_kernel(slot, in_ref, out_ref):
    rows = in_ref.shape[1] // 2
    out_ref[0, 0, 0] = in_ref[0, :rows, :]
    out_ref[0, 1, 0] = in_ref[0, rows:, :]


def place_up(value, slot, planes):
    pieces, rows2, width = value.shape
    inner = pieces // planes
    out = pl.pallas_call(
        place_up_kernel,
        grid_spec=pltpu.PrefetchScalarGridSpec(
            num_scalar_prefetch=1,
            grid=(pieces,),
            in_specs=[pl.BlockSpec((1, rows2, width), lambda p, t: (t[p], 0, 0))],
            out_specs=pl.BlockSpec(
                (1, 2, 1, rows2 // 2, width), lambda p, t: (p // inner, 0, p % inner, 0, 0)
            ),
        ),
        out_shape=jax.ShapeDtypeStruct((planes, 2, inner, rows2 // 2, width), value.dtype),
        name="place_up",
    )(slot, value)
    return out.reshape(pieces * rows2, width)


def place_down_kernel(slot, in_ref, out_ref):
    rows, width = in_ref.shape[1], out_ref.shape[2]
    out_ref[0, :rows, :] = in_ref[0, :, :width]
    out_ref[0, rows:, :] = in_ref[0, :, width:]


def place_down(value, slot):
    pieces, rows, width2 = value.shape
    out = pl.pallas_call(
        place_down_kernel,
        grid_spec=pltpu.PrefetchScalarGridSpec(
            num_scalar_prefetch=1,
            grid=(pieces,),
            in_specs=[pl.BlockSpec((1, rows, width2), lambda p, t: (t[p], 0, 0))],
            out_specs=pl.BlockSpec((1, 2 * rows, width2 // 2), lambda p, t: (p, 0, 0)),
        ),
        out_shape=jax.ShapeDtypeStruct((pieces, 2 * rows, width2 // 2), value.dtype),
        name="place_down",
    )(slot, value)
    return out.reshape(pieces * 2 * rows, width2 // 2)


def rotate(value, cosine, sine, sign):
    lane = lax.broadcasted_iota(jnp.int32, value.shape, 1) % HEAD_DIM
    lanes = value.shape[1]
    other = jnp.where(
        lane < ROT // 2,
        pltpu.roll(value, lanes - ROT // 2, 1),
        pltpu.roll(value, ROT // 2, 1),
    )
    return value * cosine + other * (sine * sign)


def send_chunks(table_ref, held, out_refs, sems):
    count = len(out_refs)
    copies = [
        pltpu.make_async_copy(held.at[table_ref[k]], out_refs[k], sems.at[k])
        for k in range(count)
    ]
    for copy in copies:
        copy.start()
    for copy in copies:
        copy.wait()


def qkv_kernel(plan, table_ref, x_ref, w_ref, bias_ref, cos_ref, sin_ref, *rest):
    ranks, seqs, per_rank, tokens, wide = plan
    out_refs, held, sems = rest[: ranks * per_rank], rest[-2], rest[-1]
    seq_groups = seqs // per_rank
    groups = ranks // seq_groups
    rotated = 2 * wide // 3

    def step(s, carry):
        rows = pl.ds(pl.multiple_of(s * tokens, tokens), tokens)
        x = x_ref[rows, :]
        cosine, sine = cos_ref[rows, :], sin_ref[rows, :]
        for g in range(groups):
            cols = slice(g * wide, (g + 1) * wide)
            joined = dot(x, w_ref[:, cols]) + bias_ref[:, cols]
            turned = rotate(joined[:, :rotated], cosine, sine, 1.0)
            rank = g * seq_groups + s // per_rank
            held[s % per_rank, rank, :, :rotated] = turned.astype(BF16)
            held[s % per_rank, rank, :, rotated:] = joined[:, rotated:].astype(BF16)
        return carry

    lax.fori_loop(0, seqs, step, 0)
    copies = [
        pltpu.make_async_copy(
            held.at[q, table_ref[k]], out_refs[q * ranks + k], sems.at[q * ranks + k]
        )
        for q in range(per_rank)
        for k in range(ranks)
    ]
    for copy in copies:
        copy.start()
    for copy in copies:
        copy.wait()


def qkv_chunks(plan, table, x, weight, bias, cosine, sine):
    ranks, seqs, per_rank, tokens, wide = plan
    count = ranks * per_rank
    return pl.pallas_call(
        partial(qkv_kernel, plan),
        in_specs=[SMEM] + [VMEM] * 5,
        out_specs=[ANY] * count,
        out_shape=[jax.ShapeDtypeStruct((tokens, wide), BF16)] * count,
        scratch_shapes=[
            pltpu.VMEM((per_rank, ranks, tokens, wide), BF16),
            pltpu.SemaphoreType.DMA((count,)),
        ],
        compiler_params=params(40),
        cost_estimate=pl.CostEstimate(
            flops=2 * x.shape[0] * weight.shape[0] * weight.shape[1],
            bytes_accessed=12 << 20,
            transcendentals=0,
        ),
        name="qkv_chunks",
    )(table, x, weight, bias, cosine, sine)


def head_grad_kernel(plan, table_ref, x_ref, w_ref, *rest):
    ranks, seqs, per_rank, tokens, wide = plan
    out_refs, held, sems = rest[: ranks * per_rank], rest[-2], rest[-1]
    seq_groups = seqs // per_rank
    groups = ranks // seq_groups

    def step(s, carry):
        rows = pl.ds(pl.multiple_of(s * tokens, tokens), tokens)
        grads = dot(x_ref[rows, :], w_ref[...], NT).astype(BF16)
        for g in range(groups):
            held[s % per_rank, g * seq_groups + s // per_rank] = grads[:, g * wide : (g + 1) * wide]
        return carry

    lax.fori_loop(0, seqs, step, 0)
    copies = [
        pltpu.make_async_copy(
            held.at[q, table_ref[k]], out_refs[q * ranks + k], sems.at[q * ranks + k]
        )
        for q in range(per_rank)
        for k in range(ranks)
    ]
    for copy in copies:
        copy.start()
    for copy in copies:
        copy.wait()


def head_grad_chunks(plan, table, x, weight):
    ranks, seqs, per_rank, tokens, wide = plan
    count = ranks * per_rank
    return pl.pallas_call(
        partial(head_grad_kernel, plan),
        in_specs=[SMEM] + [VMEM] * 2,
        out_specs=[ANY] * count,
        out_shape=[jax.ShapeDtypeStruct((tokens, wide), BF16)] * count,
        scratch_shapes=[
            pltpu.VMEM((per_rank, ranks, tokens, wide), BF16),
            pltpu.SemaphoreType.DMA((count,)),
        ],
        compiler_params=params(32),
        cost_estimate=pl.CostEstimate(
            flops=2 * x.shape[0] * weight.shape[0] * weight.shape[1],
            bytes_accessed=4 << 20,
            transcendentals=0,
        ),
        name="head_grad_chunks",
    )(table, x, weight)


def attention_kernel(ranks, table_ref, low_ref, start_ref, *rest):
    chunk_refs = rest[:ranks]
    grad_refs = rest[ranks : 2 * ranks]
    out_refs = rest[2 * ranks : 3 * ranks]
    (chunk, grads, turned, grads_t, natural, scores, products, sums, outs, in_sems, out_sems) = rest[
        3 * ranks :
    ]
    block, wide = grads.shape[1:]
    heads = wide // HEAD_DIM
    scale = HEAD_DIM ** (-0.5)
    power = scale * LOG2_E
    copies = []
    for k in range(ranks):
        at = table_ref[k]
        copies.append(pltpu.make_async_copy(chunk_refs[k], chunk.at[at], in_sems.at[2 * k]))
        copies.append(pltpu.make_async_copy(grad_refs[k], grads.at[at], in_sems.at[2 * k + 1]))
    for copy in copies:
        copy.start()
    for copy in copies:
        copy.wait()

    def prepare(b, carry):
        triple, grad = chunk[b], grads[b]
        turned[b] = triple.T
        grads_t[b] = grad.T
        for h in range(heads):
            own = slice(h * HEAD_DIM, (h + 1) * HEAD_DIM)
            for kind in range(3):
                natural[h, kind, b] = triple[:, kind * wide : (kind + 1) * wide][:, own]
            natural[h, 3, b] = grad[:, own]
            sums[h, 0, b] = jnp.zeros((block, HEAD_DIM), F32)
            sums[h, 1, b] = jnp.zeros((block, HEAD_DIM), F32)
        return carry

    lax.fori_loop(0, ranks, prepare, 0)

    def rows_of(h, kind):
        return slice(kind * wide + h * HEAD_DIM, kind * wide + (h + 1) * HEAD_DIM)

    def queries(i, carry):
        start = start_ref[i]
        query = i * block + lax.broadcasted_iota(jnp.int32, (1, block), 1)
        low = low_ref[i]

        def score(j, tops):
            key = j * block + lax.broadcasted_iota(jnp.int32, (block, block), 0)
            allowed = (key <= query) & (key >= start)
            found = []
            for h in range(heads):
                value = dot(natural[h, 1, j], turned[i, rows_of(h, 0), :])
                value = jnp.where(allowed, value, MASKED_SCORE)
                scores[h, j] = value
                found.append(jnp.maximum(tops[h], jnp.max(value, axis=0, keepdims=True)))
            return tuple(found)

        tops = lax.fori_loop(
            low, i + 1, score, (jnp.full((1, block), MASKED_SCORE, F32),) * heads
        )

        def weigh(j, carried):
            found = []
            for h in range(heads):
                total, delta = carried[h]
                expo = jnp.exp2((scores[h, j] - tops[h]) * power)
                scores[h, j] = expo
                product = dot(natural[h, 2, j], grads_t[i, rows_of(h, 0), :])
                products[h, j] = product
                found.append(
                    (
                        total + jnp.sum(expo, axis=0, keepdims=True),
                        delta + jnp.sum(expo * product, axis=0, keepdims=True),
                    )
                )
            return tuple(found)

        zero = jnp.zeros((1, block), F32)
        stats = lax.fori_loop(low, i + 1, weigh, ((zero, zero),) * heads)
        inverse = [1.0 / total for total, _ in stats]
        deltas = [delta * inv for (_, delta), inv in zip(stats, inverse)]

        def collect(j, carried):
            found = []
            for h in range(heads):
                mixed, query_grad = carried[h]
                prob = scores[h, j] * inverse[h]
                rounded = prob.astype(BF16)
                slope = (prob * (products[h, j] - deltas[h])).astype(BF16)
                mixed = mixed + dot(turned[j, rows_of(h, 2), :], rounded)
                query_grad = query_grad + dot(turned[j, rows_of(h, 1), :], slope)
                sums[h, 0, j] += dot(slope, natural[h, 0, i])
                sums[h, 1, j] += dot(rounded, natural[h, 3, i])
                found.append((mixed, query_grad))
            return tuple(found)

        empty = jnp.zeros((HEAD_DIM, block), F32)
        totals = lax.fori_loop(low, i + 1, collect, ((empty, empty),) * heads)
        mixed = jnp.concatenate([t[0] for t in totals], axis=0)
        query_grad = jnp.concatenate([t[1] for t in totals], axis=0)
        outs[i, :, :wide] = mixed.T.astype(BF16)
        outs[i, :, wide : 2 * wide] = (query_grad * scale).T.astype(BF16)
        return carry

    lax.fori_loop(0, ranks, queries, 0)

    def finish(b, carry):
        for kind in range(2):
            value = jnp.concatenate([sums[h, kind, b] for h in range(heads)], axis=1)
            if kind == 0:
                value = value * scale
            outs[b, :, (2 + kind) * wide : (3 + kind) * wide] = value.astype(BF16)
        return carry

    lax.fori_loop(0, ranks, finish, 0)
    send_chunks(table_ref, outs, out_refs, out_sems)


def attention(table, low, start, chunks, grads):
    ranks = len(chunks)
    block, wide = grads[0].shape
    heads = wide // HEAD_DIM
    pairs = ranks * (ranks + 1) // 2 * block * block * heads
    return pl.pallas_call(
        partial(attention_kernel, ranks),
        in_specs=[SMEM, SMEM, VMEM] + [ANY] * (2 * ranks),
        out_specs=[ANY] * ranks,
        out_shape=[jax.ShapeDtypeStruct((block, 4 * wide), BF16)] * ranks,
        scratch_shapes=[
            pltpu.VMEM((ranks, block, 3 * wide), BF16),
            pltpu.VMEM((ranks, block, wide), BF16),
            pltpu.VMEM((ranks, 3 * wide, block), BF16),
            pltpu.VMEM((ranks, wide, block), BF16),
            pltpu.VMEM((heads, 4, ranks, block, HEAD_DIM), BF16),
            pltpu.VMEM((heads, ranks, block, block), F32),
            pltpu.VMEM((heads, ranks, block, block), F32),
            pltpu.VMEM((heads, 2, ranks, block, HEAD_DIM), F32),
            pltpu.VMEM((ranks, block, 4 * wide), BF16),
            pltpu.SemaphoreType.DMA((2 * ranks,)),
            pltpu.SemaphoreType.DMA((ranks,)),
        ],
        compiler_params=params(56),
        cost_estimate=pl.CostEstimate(
            flops=2 * 6 * 4 * HEAD_DIM * pairs,
            bytes_accessed=8 * ranks * block * wide * 2,
            transcendentals=pairs,
        ),
        name="attention",
    )(table, low, start, *chunks, *grads)


def return_kernel(plan, table_ref, cos_ref, sin_ref, *rest):
    ranks, seqs, per_rank, tokens, wide = plan
    count = ranks * per_rank
    in_refs = rest[:count]
    mixed_ref, grad_ref, held, sems = rest[count:]
    seq_groups = seqs // per_rank
    groups = ranks // seq_groups
    copies = [
        pltpu.make_async_copy(
            in_refs[q * ranks + k], held.at[q, table_ref[k]], sems.at[q * ranks + k]
        )
        for q in range(per_rank)
        for k in range(ranks)
    ]
    for copy in copies:
        copy.start()
    for copy in copies:
        copy.wait()

    def step(s, carry):
        rows = pl.ds(pl.multiple_of(s * tokens, tokens), tokens)
        cosine, sine = cos_ref[rows, :], sin_ref[rows, :]
        for g in range(groups):
            value = held[s % per_rank, g * seq_groups + s // per_rank]
            mixed_ref[rows, g * wide : (g + 1) * wide] = value[:, :wide]
            turned = rotate(value[:, wide : 3 * wide].astype(F32), cosine, sine, -1.0)
            at = 3 * g * wide
            grad_ref[rows, at : at + 2 * wide] = turned.astype(BF16)
            grad_ref[rows, at + 2 * wide : at + 3 * wide] = value[:, 3 * wide :]
        return carry

    lax.fori_loop(0, seqs, step, 0)


def return_chunks(plan, table, cosine, sine, chunks):
    ranks, seqs, per_rank, tokens, wide = plan
    groups = ranks * per_rank // seqs
    return pl.pallas_call(
        partial(return_kernel, plan),
        in_specs=[SMEM, VMEM, VMEM] + [ANY] * len(chunks),
        out_specs=[VMEM, VMEM],
        out_shape=[
            jax.ShapeDtypeStruct((seqs * tokens, groups * wide), BF16),
            jax.ShapeDtypeStruct((seqs * tokens, 3 * groups * wide), BF16),
        ],
        scratch_shapes=[
            pltpu.VMEM((per_rank, ranks, tokens, 4 * wide), BF16),
            pltpu.SemaphoreType.DMA((len(chunks),)),
        ],
        compiler_params=params(40),
        cost_estimate=pl.CostEstimate(
            flops=8 * seqs * tokens * 4 * groups * wide, bytes_accessed=12 << 20, transcendentals=0
        ),
        name="return_chunks",
    )(table, cosine, sine, *chunks)


def on_device(
    hidden,
    positions,
    ln1_gain,
    ln1_bias,
    ln2_gain,
    ln2_bias,
    qkv_weight,
    qkv_bias,
    dense_weight,
    dense_bias,
    up_weight,
    up_bias,
    down_weight,
    down_bias,
    cotangent,
):
    seq_dp, tokens, width = hidden.shape
    ulysses, blk, dp = lax.axis_size("ulysses"), lax.axis_size("blk"), lax.axis_size("dp")
    planes = dp // 2
    ranks = blk * ulysses
    core = lax.axis_index("dp") % 2
    rank = lax.axis_index("blk") * ulysses + lax.axis_index("ulysses")
    mine = (lax.axis_index("dp") // 2) * ranks + rank
    devices = dp * ranks
    half_rows = seq_dp * tokens
    rows = 2 * half_rows
    piece = width // devices
    ff = up_weight.shape[1]

    seqs = 2 * seq_dp
    pairs = seqs * (HEADS // 2) // ranks
    heads_each = 2 if pairs % 2 == 0 else 1
    seqs_each = pairs // heads_each
    seq_groups = seqs // seqs_each
    groups = HEADS // 2 // heads_each
    wide = heads_each * HEAD_DIM
    table = rank ^ jnp.arange(ranks, dtype=jnp.int32)

    def with_partner(value):
        return jnp.concatenate([value, swap(value, "dp", 1)], axis=0)

    stage_z = [("ulysses", bit) for bit in reversed(bits_of(ulysses))]
    stage_y = [("blk", bit) for bit in bits_of(blk)]
    stage_x = [("dp", bit) for bit in bits_of(dp)[1:]]
    order_a, order_b = stage_z + stage_y + stage_x, stage_z + stage_x + stage_y

    def core_columns(value, lead, index):
        value = value.reshape(lead, 3, planes, 2, HEADS // dp // heads_each, wide)
        value = pick(value, index, 3)
        return value.transpose(0, 2, 3, 1, 4).reshape(lead, 3 * width // 2)

    def core_ff(value, lead, index):
        return pick(value.reshape(lead, planes, 2, ff // dp), index, 2).reshape(lead, ff // 2)

    def both_cores(kept, sent):
        came = swap(sent, "dp", 1)
        return jnp.concatenate(
            [jnp.where(core == 0, kept, came), jnp.where(core == 0, came, kept)], axis=0
        )

    qkv_piece = both_cores(
        core_columns(qkv_weight, piece, core), core_columns(qkv_weight, piece, 1 - core)
    )
    dense_piece = jnp.concatenate(
        [dense_weight[:, : width // 2], dense_weight[:, width // 2 :]], axis=0
    )
    first = gather(jnp.concatenate([qkv_piece, dense_piece], axis=1)[None], stage_z)
    first_a = gather(first[..., :width], stage_y + stage_x)
    first_b = gather(first[..., width:], stage_x + stage_y)
    slot_a, slot_b = slots_of(order_a, mine), slots_of(order_b, mine)
    qkv_full, dense_full = place_qkv(first_a, first_b, slot_a, slot_b, planes)

    small = [ln1_gain, ln1_bias, ln2_gain, ln2_bias, qkv_bias, dense_bias, up_bias, down_bias]
    sizes = [value.shape[0] for value in small]
    length = sum(sizes)
    padded = -(-length // 128) * 128
    packed = jnp.concatenate(small + [jnp.zeros((padded - length,), BF16)])[None]
    packed = gather(packed, [("dp", 1)] + stage_z + stage_y + stage_x)
    relative = jnp.zeros((devices,), jnp.int32)
    weights = [ranks] + [
        natural_weight(axis, bit) * (2 if axis == "dp" else 1)
        for axis, bit in stage_z + stage_y + stage_x
    ]
    for at, weight in enumerate(weights):
        relative = relative + ((jnp.arange(devices, dtype=jnp.int32) >> at) % 2) * weight
    home = (lax.axis_index("dp") * ranks + rank) ^ relative
    sorting = (jnp.arange(devices, dtype=jnp.int32)[:, None] == home[None, :]).astype(BF16)
    packed = dot(sorting, packed)
    vectors, at = [], 0
    for size in sizes:
        vectors.append(packed[:, at : at + size].reshape(-1))
        at += size
    gain_one, bias_one, gain_two, bias_two, qkv_shift, dense_shift, up_shift, down_shift = vectors
    qkv_shift = core_columns(qkv_shift, 1, core)
    up_shift = core_ff(up_shift, 1, core)

    inputs = with_partner(hidden.reshape(half_rows, width))
    upstream = with_partner(cotangent.reshape(half_rows, width))
    places = with_partner(positions)
    wide_inputs = inputs.astype(F32)
    center = wide_inputs - jnp.mean(wide_inputs, axis=-1, keepdims=True)
    spread = lax.rsqrt(jnp.mean(center * center, axis=-1, keepdims=True) + EPSILON)
    normal = center * spread
    norm1 = (normal * gain_one + bias_one).astype(BF16)
    norm2 = (normal * gain_two + bias_two).astype(BF16)

    own_places = lax.dynamic_slice_in_dim(
        places, lax.axis_index("ulysses") * tokens, tokens, 1
    ).reshape(rows, 1)
    lane = jnp.arange(2 * wide, dtype=jnp.int32) % HEAD_DIM
    freqs = 10000.0 ** (-((lane % (ROT // 2)).astype(F32) * 2.0 / ROT))
    freqs = jnp.where(lane < ROT, freqs, 0.0)
    angles = own_places.astype(F32) * freqs
    cosine = jnp.cos(angles)
    sine = jnp.sin(angles) * jnp.where(lane < ROT // 2, -1.0, 1.0)

    every = gather(places[None], stage_y)
    here = lax.axis_index("blk")
    every = jnp.stack([pick(every, here ^ j, 0) for j in range(blk)], axis=1)
    every = every.reshape(seqs, ranks * tokens)
    starts = jnp.arange(ranks * tokens, dtype=jnp.int32) - every
    starts = pick(starts.reshape(seq_groups, seqs_each, ranks, 1, tokens), rank % seq_groups, 0)
    lows = starts[:, :, 0, 0] // tokens

    def exchange(buffers):
        return [buffers[0]] + [swap(buffers[k], RANKS, k) for k in range(1, ranks)]

    def by_seq(buffers):
        return [buffers[q * ranks : (q + 1) * ranks] for q in range(seqs_each)]

    plan = (ranks, seqs, seqs_each, tokens, wide)
    plan3 = (ranks, seqs, seqs_each, tokens, 3 * wide)
    sent_grads = by_seq(head_grad_chunks(plan, table, upstream, dense_full))
    sent_chunks = by_seq(qkv_chunks(plan3, table, norm1, qkv_full, qkv_shift, cosine, sine))
    returned = []
    for q in range(seqs_each):
        grads = exchange(sent_grads[q])
        chunks = exchange(sent_chunks[q])
        returned += exchange(attention(table, lows[q], starts[q], chunks, grads))
    mixed, joined_grad = return_chunks(plan, table, cosine, sine, returned)

    up_piece = both_cores(core_ff(up_weight, piece, core), core_ff(up_weight, piece, 1 - core))
    down_rows = down_weight.shape[0] // 2
    down_piece = jnp.concatenate([down_weight[:down_rows], down_weight[down_rows:]], axis=1)
    up_full = place_up(gather(up_piece[None], order_a), slot_a, planes)
    down_full = place_down(gather(down_piece[None], order_b), slot_b)
    up_pre = dot(norm2, up_full) + up_shift
    active, gelu_back = jax.vjp(partial(jax.nn.gelu, approximate=False), up_pre)
    active = active.astype(BF16)
    up_grad = gelu_back(dot(upstream, down_full, NT))[0].astype(BF16)
    norm2_grad = dot(up_grad, up_full, NT)

    def first_stage(left, right, axis, bit, dims, dim):
        left = left.reshape((rows,) + dims)
        mine_bit = own_bit(axis, bit)
        outer = dims[:dim] + dims[dim + 1 :]

        def product(index):
            return dot(pick(left, index, dim + 1).reshape(rows, -1), right, TN)

        sent = product(1 - mine_bit).astype(BF16)
        total = product(mine_bit) + swap(sent, axis, bit).astype(F32)
        return total.reshape(outer + right.shape[1:])

    bits = [("dp", bit) for bit in reversed(bits_of(dp)[1:])]
    bits += [("blk", bit) for bit in reversed(bits_of(blk))]
    bits += [("ulysses", bit) for bit in reversed(bits_of(ulysses))]
    low_z = list(reversed(stage_z))

    def reduce_rows(left, right, order, with_core):
        names = list(bits)
        if with_core:
            names.insert(len(stage_x), ("dp", 1))
        unit = left.shape[1] >> len(names)
        dims = (2,) * len(names) + (unit,)
        total = None
        for axis, bit in order:
            dim = names.index((axis, bit))
            if total is None:
                total = first_stage(left, right, axis, bit, dims, dim)
            else:
                total = reduce_stage(total, dim, axis, bit)
            names.pop(dim)
        if with_core:
            total = jnp.where(core == 0, total, total[::-1])
        return total

    xyz, yxz = stage_x + stage_y + low_z, stage_y + stage_x + low_z
    down_w_grad = reduce_rows(active, upstream, yxz, False)
    up_w_grad = reduce_rows(norm2, up_grad, xyz, True)
    dense_w_grad = reduce_rows(mixed, upstream, xyz, False)
    cut = joined_grad.shape[1] // 2
    qkv_a = reduce_rows(norm1, joined_grad[:, :cut], xyz, True)
    qkv_b = reduce_rows(norm1, joined_grad[:, cut:], yxz, True)
    norm1_grad = dot(joined_grad, qkv_full, NT)

    def columns_home(total, kinds):
        other = swap(total[1], "dp", 1)
        kept = total[0]
        pair = [jnp.where(core == 0, kept, other), jnp.where(core == 0, other, kept)]
        lead = kept.shape[0]
        if kinds == 1:
            pair = [value.reshape(lead, planes, ff // dp) for value in pair]
            return jnp.stack(pair, axis=2).reshape(lead, ff)
        inner = HEADS // dp // heads_each
        pair = [
            value.reshape(lead, planes, inner, 3, wide).transpose(0, 3, 1, 2, 4) for value in pair
        ]
        return jnp.stack(pair, axis=3).reshape(lead, 3 * width)

    up_w_grad = columns_home(up_w_grad, 1)
    qkv_w_grad = columns_home(jnp.concatenate([qkv_a, qkv_b], axis=-1), 3)

    branch = dot(mixed, dense_full) + dot(active, down_full)
    branch = branch[:half_rows] + swap(branch[half_rows:], "dp", 1)
    output = wide_inputs[:half_rows] + (branch + dense_shift + down_shift)
    output = output.astype(BF16).reshape(hidden.shape)
    slope = norm1_grad * gain_one + norm2_grad * gain_two
    slope = slope[:half_rows] + swap(slope[half_rows:], "dp", 1)
    own = normal[:half_rows]
    term = spread[:half_rows] * (
        slope
        - jnp.mean(slope, axis=-1, keepdims=True)
        - own * jnp.mean(slope * own, axis=-1, keepdims=True)
    )
    input_grad = (upstream[:half_rows].astype(F32) + term).astype(BF16).reshape(hidden.shape)

    def spread_core(value, kinds, last):
        value = value.reshape(kinds, planes, 1, last)
        empty = jnp.zeros_like(value)
        pair = [jnp.where(core == c, value, empty) for c in range(2)]
        return jnp.concatenate(pair, axis=2).reshape(-1)

    def total_of(value):
        return jnp.sum(value.astype(F32), axis=0)

    shift_grad = total_of(upstream[:half_rows])
    inner = HEADS // dp // heads_each
    qkv_b_grad = total_of(joined_grad).reshape(planes, inner, 3, wide).transpose(2, 0, 1, 3)
    qkv_b_grad = spread_core(qkv_b_grad, 3, inner * wide)
    small_grads = [
        total_of(norm1_grad * normal),
        total_of(norm1_grad),
        total_of(norm2_grad * normal),
        total_of(norm2_grad),
        qkv_b_grad,
        shift_grad,
        spread_core(total_of(up_grad), 1, ff // dp),
    ]
    small_sizes = [value.shape[0] // devices for value in small_grads]
    total = jnp.concatenate([value.reshape(devices, -1) for value in small_grads], axis=1)
    total = jnp.pad(total, ((0, 0), (0, -total.shape[1] % 128)))
    names = list(bits)
    names.insert(len(stage_x), ("dp", 1))
    total = total.reshape((2,) * len(names) + (1, -1))
    for axis, bit in xyz + [("dp", 1)]:
        dim = names.index((axis, bit))
        total = reduce_stage(total, dim, axis, bit, F32)
        names.pop(dim)
    total = total.reshape(-1)
    smalls, at = [], 0
    for size in small_sizes:
        smalls.append(total[at : at + size])
        at += size
    return (
        output,
        input_grad,
        smalls[0],
        smalls[1],
        smalls[2],
        smalls[3],
        qkv_w_grad,
        smalls[4],
        dense_w_grad,
        smalls[5],
        up_w_grad,
        smalls[6],
        down_w_grad,
        smalls[5],
    )


def solution(mesh):
    rows = ("dp", "blk", "ulysses")
    tokens = P("dp", ("blk", "ulysses"), None)
    vector, matrix = P(rows), P(rows, None)
    in_specs = (tokens, P("dp", "blk")) + (vector,) * 4 + (matrix, vector) * 4 + (tokens,)
    out_specs = (tokens, tokens) + (vector,) * 4 + (matrix, vector) * 4
    return jax.shard_map(
        on_device, mesh=mesh, in_specs=in_specs, out_specs=out_specs, check_vma=False
    )
```

```python
from functools import partial

import jax
import jax.numpy as jnp
from jax import lax
from jax.experimental import pallas as pl
from jax.experimental.pallas import tpu as pltpu
from jax.sharding import PartitionSpec as P

HEADS = 16
HEAD_DIM = 64
ROT = 16
EPSILON = 1e-05
MASKED_SCORE = -1e30
LOG2_E = 1.4426950408889634
RANKS = ("blk", "ulysses")
F32 = jnp.float32
BF16 = jnp.bfloat16
NN = (((1,), (0,)), ((), ()))
NT = (((1,), (1,)), ((), ()))
TN = (((0,), (0,)), ((), ()))
ANY = pl.BlockSpec(memory_space=pl.ANY)
VMEM = pl.BlockSpec(memory_space=pltpu.VMEM)
SMEM = pl.BlockSpec(memory_space=pltpu.SMEM)


def dot(left, right, dims=NN):
    return lax.dot_general(left, right, dims, preferred_element_type=F32)


def swap(value, axis, bit):
    size = lax.axis_size(axis)
    return lax.ppermute(value, axis, [(i, i ^ bit) for i in range(size)])


def bits_of(size):
    return [1 << k for k in range(size.bit_length() - 1)]


def gather(value, stages):
    for axis, bit in stages:
        value = jnp.concatenate([value, swap(value, axis, bit)], axis=0)
    return value


def after(value, other):
    return lax.optimization_barrier((value, other))[0]


def gather_pair(value, stages):
    value = gather(value, stages[:-1])
    return [value, swap(value, *stages[-1])]


def natural_weight(axis, bit):
    ulysses = lax.axis_size("ulysses")
    if axis == "ulysses":
        return bit
    if axis == "blk":
        return bit * ulysses
    return (bit // 2) * ulysses * lax.axis_size("blk")


def places_of(stages, mine):
    slot = jnp.arange(1 << len(stages), dtype=jnp.int32)
    relative = jnp.zeros_like(slot)
    for at, (axis, bit) in enumerate(stages):
        relative = relative + ((slot >> at) % 2) * natural_weight(axis, bit)
    return relative ^ mine


def own_bit(axis, bit):
    return (lax.axis_index(axis) // bit) % 2


def pick(value, index, dim):
    return lax.dynamic_index_in_dim(value, index, dim, keepdims=False)


def reduce_stage(total, dim, axis, bit, wire=BF16):
    mine = own_bit(axis, bit)
    sent = pick(total, 1 - mine, dim).astype(wire)
    return pick(total, mine, dim) + swap(sent, axis, bit).astype(F32)


def params(mib):
    return pltpu.CompilerParams(vmem_limit_bytes=mib << 20)


class Sems:
    def __init__(self, array):
        self.array, self.used = array, 0

    def copy(self, source, target):
        self.used += 1
        return pltpu.make_async_copy(source, target, self.array.at[self.used - 1])


def run(copies):
    for copy in copies:
        copy.start()
    for copy in copies:
        copy.wait()


def slot_refs(refs):
    return [ref.at[at] for ref in refs for at in range(ref.shape[0])]


def in_order(buffers, places, direct):
    if direct:
        return buffers, places
    natural = jnp.arange(places.shape[0], dtype=jnp.int32)
    whole = jnp.concatenate(buffers, axis=0)
    return [jnp.take(whole, jnp.argsort(places), axis=0)], natural


def rotate(value, cosine, sine, sign):
    lane = lax.broadcasted_iota(jnp.int32, value.shape, 1) % HEAD_DIM
    lanes = value.shape[1]
    other = jnp.where(
        lane < ROT // 2,
        pltpu.roll(value, lanes - ROT // 2, 1),
        pltpu.roll(value, ROT // 2, 1),
    )
    return value * cosine + other * (sine * sign)


def first_kernel(plan, places, counts, place_a, place_b, *rest):
    ranks, seqs, per_rank, tokens, wide = plan
    planes, inner, piece = places
    x_ref, cot_ref, bias_ref, cos_ref, sin_ref = rest[:5]
    a_refs, b_refs = rest[5 : 5 + counts[0]], rest[5 + counts[0] : 5 + sum(counts)]
    rest = rest[5 + sum(counts) :]
    out_refs, (w_ref, dense_ref, in_sems) = rest[:per_rank], rest[per_rank:]
    seq_groups = seqs // per_rank
    groups = ranks // seq_groups
    width = x_ref.shape[1]
    half = width // 2
    give = Sems(in_sems)
    copies = []
    for slots, place_ref, second in ((a_refs, place_a, False), (b_refs, place_b, True)):
        for at, slot in enumerate(slot_refs(slots)):
            place = place_ref[at]
            for part in range(2):
                source = slot.at[pl.ds(part * piece, piece)]
                row = ((place // inner) * 2 + part) * inner + place % inner
                span = pl.ds(pl.multiple_of(row * piece, piece), piece)
                if second:
                    own = pl.ds(pl.multiple_of(place * piece, piece), piece)
                    copies.append(
                        give.copy(source.at[:, pl.ds(0, half)], w_ref.at[span, pl.ds(width, half)])
                    )
                    copies.append(
                        give.copy(
                            source.at[:, pl.ds(half, half)],
                            dense_ref.at[own, pl.ds(part * half, half)],
                        )
                    )
                else:
                    copies.append(give.copy(source, w_ref.at[span, pl.ds(0, width)]))
    run(copies)

    for q in range(per_rank):
        held = out_refs[q]

        def step(group, carry):
            rows = pl.ds(pl.multiple_of((group * per_rank + q) * tokens, tokens), tokens)
            x = x_ref[rows, :]
            cosine, sine = cos_ref[rows, :], sin_ref[rows, :]
            grads = dot(cot_ref[rows, :], dense_ref[...], NT).astype(BF16)
            for g in range(groups):
                cols = slice(3 * g * wide, 3 * (g + 1) * wide)
                joined = dot(x, w_ref[:, cols]) + bias_ref[:, cols]
                turned = rotate(joined[:, : 2 * wide], cosine, sine, 1.0)
                rank = g * seq_groups + group
                held[rank, :, : 2 * wide] = turned.astype(BF16)
                held[rank, :, 2 * wide : 3 * wide] = joined[:, 2 * wide :].astype(BF16)
                held[rank, :, 3 * wide :] = grads[:, g * wide : (g + 1) * wide]
            return carry

        lax.fori_loop(0, seq_groups, step, 0)


def first_chunks(plan, places, a, b, place_a, place_b, x, cot, bias, cosine, sine):
    ranks, seqs, per_rank, tokens, wide = plan
    width = x.shape[1]
    slots = place_a.shape[0]
    outs = pl.pallas_call(
        partial(first_kernel, plan, places, (len(a), len(b))),
        in_specs=[SMEM] * 2 + [VMEM] * 5 + [ANY] * (len(a) + len(b)),
        out_specs=[VMEM] * (per_rank + 2),
        out_shape=[jax.ShapeDtypeStruct((ranks, tokens, 4 * wide), BF16)] * per_rank
        + [
            jax.ShapeDtypeStruct((width, 3 * width // 2), BF16),
            jax.ShapeDtypeStruct((width // 2, width), BF16),
        ],
        scratch_shapes=[pltpu.SemaphoreType.DMA((6 * slots,))],
        compiler_params=params(48),
        cost_estimate=pl.CostEstimate(
            flops=4 * x.shape[0] * width * width, bytes_accessed=20 << 20, transcendentals=0
        ),
        name="first_chunks",
    )(place_a, place_b, x, cot, bias, cosine, sine, *a, *b)
    return outs[:per_rank], outs[per_rank], outs[per_rank + 1]


def feed_kernel(places, counts, block, side_unit, up_place, down_place, half_ref, x_ref, cot_ref, bias_ref, *rest):
    planes, inner, piece = places
    up_refs, down_refs = rest[: counts[0]], rest[counts[0] : sum(counts)]
    rest = rest[sum(counts) :]
    up_send, up_keep, down_send, down_keep, out_ref, norm_ref, sum_ref = rest[:7]
    up_w, down_w, act, grad, up_s, up_k, down_s, down_k, in_sems, sems = rest[7:]
    rows, width = x_ref.shape
    ff = down_w.shape[0]
    blocks = ff // block
    tile = rows // 2
    give = Sems(in_sems)
    copies = []
    for at, slot in enumerate(slot_refs(up_refs)):
        place = up_place[at]
        for part in range(2):
            row = ((place // inner) * 2 + part) * inner + place % inner
            span = pl.ds(pl.multiple_of(row * piece, piece), piece)
            copies.append(give.copy(slot.at[pl.ds(part * piece, piece)], up_w.at[span]))
    unit = down_refs[0].shape[1]
    for at, slot in enumerate(slot_refs(down_refs)):
        span = pl.ds(pl.multiple_of(down_place[at] * unit, unit), unit)
        copies.append(give.copy(slot, down_w.at[span]))
    run(copies)
    mine, mine_block = half_ref[0], half_ref[1]
    span_half = pl.ds(pl.multiple_of(mine * (width // 2), width // 2), width // 2)
    span_other = pl.ds(pl.multiple_of((1 - mine) * (width // 2), width // 2), width // 2)

    def out_copies(step):
        cols = pl.ds(pl.multiple_of(natural(step) * block, block), block)
        at = step % (blocks // 2)
        span = pl.ds(pl.multiple_of(at * block, block), block)
        return [
            pltpu.make_async_copy(up_s.at[step], up_send.at[:, cols], sems.at[0, step]),
            pltpu.make_async_copy(up_k.at[step], up_keep.at[:, cols], sems.at[1, step]),
        ], span

    def natural(step):
        side = jnp.where(step < blocks // 2, 1 - mine_block, mine_block)
        at = step % (blocks // 2)
        return ((at // side_unit) * 2 + side) * side_unit + at % side_unit

    def one(step, carry):
        at = natural(step)
        cols = pl.ds(pl.multiple_of(at * block, block), block)
        up_b = up_w[:, cols]
        down_b = down_w[cols, :]
        bias = bias_ref[:, cols]
        for r in range(2):
            span = slice(r * tile, (r + 1) * tile)
            pre = dot(x_ref[span, :], up_b) + bias
            cdf = 0.5 * (1.0 + lax.erf(pre * (0.5**0.5)))
            slope = cdf + pre * (jnp.exp2(pre * pre * (-0.5 * LOG2_E)) * 0.3989422804014327)
            active = (pre * cdf).astype(BF16)
            act[span, :] = active
            back = (dot(cot_ref[span, :], down_b, NT) * slope).astype(BF16)
            grad[span, :] = back
            out = dot(active, down_b)
            norm = dot(back, up_b, NT)

            @pl.when(step == 0)
            def _():
                out_ref[span, :] = out
                norm_ref[span, :] = norm

            @pl.when(step > 0)
            def _():
                out_ref[span, :] += out
                norm_ref[span, :] += norm

        sum_ref[:, cols] = jnp.sum(grad[...].astype(F32), axis=0, keepdims=True)
        up_g = dot(x_ref[:, span_other], grad[...], TN)
        up_s[step] = up_g.astype(BF16)
        up_k[step] = dot(x_ref[:, span_half], grad[...], TN)
        pair, span = out_copies(step)
        for copy in pair:
            copy.start()
        down_g = dot(act[...], cot_ref[...], TN)

        @pl.when(step < blocks // 2)
        def _():
            down_s[step] = down_g.astype(BF16)
            pltpu.make_async_copy(down_s.at[step], down_send.at[span], sems.at[2, step]).start()

        @pl.when(step >= blocks // 2)
        def _():
            here = step - blocks // 2
            down_k[here] = down_g
            pltpu.make_async_copy(down_k.at[here], down_keep.at[span], sems.at[2, step]).start()

        return carry

    lax.fori_loop(0, blocks, one, 0)
    for step in range(blocks):
        pair, span = out_copies(step)
        for copy in pair:
            copy.wait()
        if step < blocks // 2:
            pltpu.make_async_copy(down_s.at[step], down_send.at[span], sems.at[2, step]).wait()
        else:
            here = step - blocks // 2
            pltpu.make_async_copy(down_k.at[here], down_keep.at[span], sems.at[2, step]).wait()


def feed_forward(places, half, x, cot, bias, up, up_place, down, down_place):
    rows, width = x.shape
    ff = bias.shape[1]
    block = min(256, ff // 2)
    blocks = ff // block
    return pl.pallas_call(
        partial(feed_kernel, places, (len(up), len(down)), block, blocks // (2 * places[0])),
        in_specs=[SMEM] * 3 + [VMEM] * 3 + [ANY] * (len(up) + len(down)),
        out_specs=[ANY] * 4 + [VMEM] * 3,
        out_shape=[
            jax.ShapeDtypeStruct((width // 2, ff), BF16),
            jax.ShapeDtypeStruct((width // 2, ff), F32),
            jax.ShapeDtypeStruct((ff // 2, width), BF16),
            jax.ShapeDtypeStruct((ff // 2, width), F32),
            jax.ShapeDtypeStruct((rows, width), F32),
            jax.ShapeDtypeStruct((rows, width), F32),
            jax.ShapeDtypeStruct((1, ff), F32),
        ],
        scratch_shapes=[
            pltpu.VMEM((width, ff), BF16),
            pltpu.VMEM((ff, width), BF16),
            pltpu.VMEM((rows, block), BF16),
            pltpu.VMEM((rows, block), BF16),
            pltpu.VMEM((blocks, width // 2, block), BF16),
            pltpu.VMEM((blocks, width // 2, block), F32),
            pltpu.VMEM((blocks // 2, block, width), BF16),
            pltpu.VMEM((blocks // 2, block, width), F32),
            pltpu.SemaphoreType.DMA((2 * up_place.shape[0] + down_place.shape[0],)),
            pltpu.SemaphoreType.DMA((3, blocks)),
        ],
        compiler_params=params(58),
        cost_estimate=pl.CostEstimate(
            flops=12 * rows * width * ff, bytes_accessed=32 << 20, transcendentals=2 * rows * ff
        ),
        name="feed_forward",
    )(up_place, down_place, half, x, cot, bias, *up, *down)


def attention_kernel(low_ref, start_ref, chunk, *rest):
    outs, turned, natural, scores, products, sums = rest
    ranks, block, wide = chunk.shape[0], chunk.shape[1], chunk.shape[2] // 4
    heads = wide // HEAD_DIM
    scale = HEAD_DIM ** (-0.5)
    power = scale * LOG2_E
    def prepare(b, carry):
        kinds = chunk[b]
        turned[b] = kinds.T
        for h in range(heads):
            own = slice(h * HEAD_DIM, (h + 1) * HEAD_DIM)
            for kind in range(4):
                natural[h, kind, b] = kinds[:, kind * wide : (kind + 1) * wide][:, own]
            sums[h, 0, b] = jnp.zeros((block, HEAD_DIM), F32)
            sums[h, 1, b] = jnp.zeros((block, HEAD_DIM), F32)
        return carry

    lax.fori_loop(0, ranks, prepare, 0)

    def rows_of(h, kind):
        return slice(kind * wide + h * HEAD_DIM, kind * wide + (h + 1) * HEAD_DIM)

    def queries(i, carry):
        start = start_ref[i]
        query = i * block + lax.broadcasted_iota(jnp.int32, (1, block), 1)
        low = low_ref[i]

        def score(j, tops):
            key = j * block + lax.broadcasted_iota(jnp.int32, (block, block), 0)
            allowed = (key <= query) & (key >= start)
            found = []
            for h in range(heads):
                value = dot(natural[h, 1, j], turned[i, rows_of(h, 0), :])
                value = jnp.where(allowed, value, MASKED_SCORE)
                scores[h, j] = value
                found.append(jnp.maximum(tops[h], jnp.max(value, axis=0, keepdims=True)))
            return tuple(found)

        tops = lax.fori_loop(
            low, i + 1, score, (jnp.full((1, block), MASKED_SCORE, F32),) * heads
        )

        def weigh(j, carried):
            found = []
            for h in range(heads):
                total, delta = carried[h]
                expo = jnp.exp2((scores[h, j] - tops[h]) * power)
                scores[h, j] = expo
                product = dot(natural[h, 2, j], turned[i, rows_of(h, 3), :])
                products[h, j] = product
                found.append(
                    (
                        total + jnp.sum(expo, axis=0, keepdims=True),
                        delta + jnp.sum(expo * product, axis=0, keepdims=True),
                    )
                )
            return tuple(found)

        zero = jnp.zeros((1, block), F32)
        stats = lax.fori_loop(low, i + 1, weigh, ((zero, zero),) * heads)
        inverse = [1.0 / total for total, _ in stats]
        deltas = [delta * inv for (_, delta), inv in zip(stats, inverse)]

        def collect(j, carried):
            found = []
            for h in range(heads):
                mixed, query_grad = carried[h]
                prob = scores[h, j] * inverse[h]
                rounded = prob.astype(BF16)
                slope = (prob * (products[h, j] - deltas[h])).astype(BF16)
                mixed = mixed + dot(turned[j, rows_of(h, 2), :], rounded)
                query_grad = query_grad + dot(turned[j, rows_of(h, 1), :], slope)
                sums[h, 0, j] += dot(slope, natural[h, 0, i])
                sums[h, 1, j] += dot(rounded, natural[h, 3, i])
                found.append((mixed, query_grad))
            return tuple(found)

        empty = jnp.zeros((HEAD_DIM, block), F32)
        totals = lax.fori_loop(low, i + 1, collect, ((empty, empty),) * heads)
        mixed = jnp.concatenate([t[0] for t in totals], axis=0)
        query_grad = jnp.concatenate([t[1] for t in totals], axis=0)
        outs[i, :, :wide] = mixed.T.astype(BF16)
        outs[i, :, wide : 2 * wide] = (query_grad * scale).T.astype(BF16)
        return carry

    lax.fori_loop(0, ranks, queries, 0)

    def finish(b, carry):
        for kind in range(2):
            value = jnp.concatenate([sums[h, kind, b] for h in range(heads)], axis=1)
            if kind == 0:
                value = value * scale
            outs[b, :, (2 + kind) * wide : (3 + kind) * wide] = value.astype(BF16)
        return carry

    lax.fori_loop(0, ranks, finish, 0)


def attention(low, start, chunk):
    ranks, block, wide = chunk.shape[0], chunk.shape[1], chunk.shape[2] // 4
    heads = wide // HEAD_DIM
    pairs = ranks * (ranks + 1) // 2 * block * block * heads
    return pl.pallas_call(
        attention_kernel,
        in_specs=[SMEM, VMEM, VMEM],
        out_specs=VMEM,
        out_shape=jax.ShapeDtypeStruct(chunk.shape, BF16),
        scratch_shapes=[
            pltpu.VMEM((ranks, 4 * wide, block), BF16),
            pltpu.VMEM((heads, 4, ranks, block, HEAD_DIM), BF16),
            pltpu.VMEM((heads, ranks, block, block), F32),
            pltpu.VMEM((heads, ranks, block, block), F32),
            pltpu.VMEM((heads, 2, ranks, block, HEAD_DIM), F32),
        ],
        compiler_params=params(56),
        cost_estimate=pl.CostEstimate(
            flops=2 * 6 * 4 * HEAD_DIM * pairs,
            bytes_accessed=8 * ranks * block * wide * 2,
            transcendentals=pairs,
        ),
        name="attention",
    )(low, start, chunk)


def return_kernel(plan, cos_ref, sin_ref, *rest):
    ranks, seqs, per_rank, tokens, wide = plan
    in_refs, (mixed_ref, grad_ref) = rest[:per_rank], rest[per_rank:]
    seq_groups = seqs // per_rank
    groups = ranks // seq_groups
    for q in range(per_rank):
        held = in_refs[q]

        def step(group, carry):
            rows = pl.ds(pl.multiple_of((group * per_rank + q) * tokens, tokens), tokens)
            cosine, sine = cos_ref[rows, :], sin_ref[rows, :]
            for g in range(groups):
                value = held[g * seq_groups + group]
                mixed_ref[rows, g * wide : (g + 1) * wide] = value[:, :wide]
                turned = rotate(value[:, wide : 3 * wide].astype(F32), cosine, sine, -1.0)
                at = 3 * g * wide
                grad_ref[rows, at : at + 2 * wide] = turned.astype(BF16)
                grad_ref[rows, at + 2 * wide : at + 3 * wide] = value[:, 3 * wide :]
            return carry

        lax.fori_loop(0, seq_groups, step, 0)


def return_chunks(plan, cosine, sine, chunks):
    ranks, seqs, per_rank, tokens, wide = plan
    groups = ranks * per_rank // seqs
    return pl.pallas_call(
        partial(return_kernel, plan),
        in_specs=[VMEM] * (2 + per_rank),
        out_specs=[VMEM, VMEM],
        out_shape=[
            jax.ShapeDtypeStruct((seqs * tokens, groups * wide), BF16),
            jax.ShapeDtypeStruct((seqs * tokens, 3 * groups * wide), BF16),
        ],
        compiler_params=params(40),
        cost_estimate=pl.CostEstimate(
            flops=8 * seqs * tokens * 4 * groups * wide, bytes_accessed=12 << 20, transcendentals=0
        ),
        name="return_chunks",
    )(cosine, sine, *chunks)


def on_device(
    hidden,
    positions,
    ln1_gain,
    ln1_bias,
    ln2_gain,
    ln2_bias,
    qkv_weight,
    qkv_bias,
    dense_weight,
    dense_bias,
    up_weight,
    up_bias,
    down_weight,
    down_bias,
    cotangent,
):
    seq_dp, tokens, width = hidden.shape
    ulysses, blk, dp = lax.axis_size("ulysses"), lax.axis_size("blk"), lax.axis_size("dp")
    planes = dp // 2
    ranks = blk * ulysses
    core = lax.axis_index("dp") % 2
    rank = lax.axis_index("blk") * ulysses + lax.axis_index("ulysses")
    mine = (lax.axis_index("dp") // 2) * ranks + rank
    devices = dp * ranks
    half_rows = seq_dp * tokens
    rows = 2 * half_rows
    piece = width // devices
    ff = up_weight.shape[1]

    seqs = 2 * seq_dp
    pairs = seqs * (HEADS // 2) // ranks
    heads_each = 2 if pairs % 2 == 0 else 1
    seqs_each = pairs // heads_each
    seq_groups = seqs // seqs_each
    groups = HEADS // 2 // heads_each
    wide = heads_each * HEAD_DIM

    def with_partner(value):
        return jnp.concatenate([value, swap(value, "dp", 1)], axis=0)

    stage_z = [("ulysses", bit) for bit in reversed(bits_of(ulysses))]
    stage_y = [("blk", bit) for bit in bits_of(blk)]
    stage_x = [("dp", bit) for bit in bits_of(dp)[1:]]
    order_a, order_b = stage_z + stage_y + stage_x, stage_z + stage_x + stage_y

    def core_columns(value, lead, index):
        value = value.reshape(lead, 3, planes, 2, HEADS // dp // heads_each, wide)
        value = pick(value, index, 3)
        return value.transpose(0, 2, 3, 1, 4).reshape(lead, 3 * width // 2)

    def core_ff(value, lead, index):
        return pick(value.reshape(lead, planes, 2, ff // dp), index, 2).reshape(lead, ff // 2)

    def both_cores(kept, sent):
        came = swap(sent, "dp", 1)
        return jnp.concatenate(
            [jnp.where(core == 0, kept, came), jnp.where(core == 0, came, kept)], axis=0
        )

    qkv_piece = both_cores(
        core_columns(qkv_weight, piece, core), core_columns(qkv_weight, piece, 1 - core)
    )
    dense_piece = jnp.concatenate(
        [dense_weight[:, : width // 2], dense_weight[:, width // 2 :]], axis=0
    )
    first = jnp.concatenate([qkv_piece, dense_piece], axis=1)[None]
    small = [ln1_gain, ln1_bias, ln2_gain, ln2_bias, qkv_bias, dense_bias, up_bias, down_bias]
    sizes = [value.shape[0] for value in small]
    length = sum(sizes)
    padded = -(-length // 128) * 128
    packed = jnp.concatenate(small + [jnp.zeros((padded - length,), BF16)])[None]
    places = with_partner(positions)
    every = gather(places[None], stage_y)
    up_piece = both_cores(core_ff(up_weight, piece, core), core_ff(up_weight, piece, 1 - core))
    up_part, down_part = up_piece[None], down_weight[None]

    packed = gather(packed, [("dp", 1)])
    beside = stage_x + stage_y
    for at, stage in enumerate(stage_z):
        packed = gather(after(packed, (first, every)), beside[at : at + 1])
        first = gather(first, [stage])
        if at == 0:
            up_part, down_part = after((up_part, down_part), first)
    up_part, down_part = gather(up_part, stage_z[:1]), gather(down_part, stage_z[:1])
    packed = gather(after(packed, first), beside[len(stage_z) :] + stage_z[:1])

    direct = piece % 16 == 0
    units = (planes, ranks, piece)
    places_a, places_b = places_of(order_a, mine), places_of(order_b, mine)
    first_a = gather_pair(first[..., :width], stage_y + stage_x)
    first_b = gather_pair(first[..., width:], stage_x + stage_y)
    packed = gather(after(packed, (first_a[0], first_b[0])), stage_z[1:])
    up_part, down_part = after((up_part, down_part), (packed, first_a[0], first_b[0]))
    up_part, down_part = gather(up_part, stage_z[1:]), gather(down_part, stage_z[1:])
    early = (up_part, down_part)
    first_a, place_a = in_order(first_a, places_a, direct)
    first_b, place_b = in_order(first_b, places_b, direct)

    relative = jnp.zeros((devices,), jnp.int32)
    weights = [ranks] + [
        natural_weight(axis, bit) * (2 if axis == "dp" else 1)
        for axis, bit in beside + stage_z
    ]
    for at, weight in enumerate(weights):
        relative = relative + ((jnp.arange(devices, dtype=jnp.int32) >> at) % 2) * weight
    home = (lax.axis_index("dp") * ranks + rank) ^ relative
    sorting = (jnp.arange(devices, dtype=jnp.int32)[:, None] == home[None, :]).astype(BF16)
    packed = dot(sorting, packed)
    vectors, at = [], 0
    for size in sizes:
        vectors.append(packed[:, at : at + size].reshape(-1))
        at += size
    gain_one, bias_one, gain_two, bias_two, qkv_shift, dense_shift, up_shift, down_shift = vectors
    qkv_shift = core_columns(qkv_shift, 1, core)
    up_shift = core_ff(up_shift, 1, core)

    inputs = with_partner(hidden.reshape(half_rows, width))
    upstream = with_partner(cotangent.reshape(half_rows, width))
    wide_inputs = inputs.astype(F32)
    center = wide_inputs - jnp.mean(wide_inputs, axis=-1, keepdims=True)
    spread = lax.rsqrt(jnp.mean(center * center, axis=-1, keepdims=True) + EPSILON)
    normal = center * spread
    norm1 = (normal * gain_one + bias_one).astype(BF16)
    norm2 = (normal * gain_two + bias_two).astype(BF16)

    own_places = lax.dynamic_slice_in_dim(
        places, lax.axis_index("ulysses") * tokens, tokens, 1
    ).reshape(rows, 1)
    lane = jnp.arange(2 * wide, dtype=jnp.int32) % HEAD_DIM
    freqs = 10000.0 ** (-((lane % (ROT // 2)).astype(F32) * 2.0 / ROT))
    freqs = jnp.where(lane < ROT, freqs, 0.0)
    angles = own_places.astype(F32) * freqs
    cosine = jnp.cos(angles)
    sine = jnp.sin(angles) * jnp.where(lane < ROT // 2, -1.0, 1.0)

    here = lax.axis_index("blk")
    every = jnp.stack([pick(every, here ^ j, 0) for j in range(blk)], axis=1)
    every = every.reshape(seqs, ranks * tokens)
    starts = jnp.arange(ranks * tokens, dtype=jnp.int32) - every
    starts = pick(starts.reshape(seq_groups, seqs_each, ranks, 1, tokens), rank % seq_groups, 0)
    lows = starts[:, :, 0, 0] // tokens

    def exchange(chunks):
        return lax.all_to_all(chunks, RANKS, split_axis=0, concat_axis=0, tiled=True)

    plan = (ranks, seqs, seqs_each, tokens, wide)
    sent, qkv_full, dense_full = first_chunks(
        plan, units, first_a, first_b, place_a, place_b,
        after(norm1, early), upstream, qkv_shift, cosine, sine,
    )
    up_part, down_part = gather(up_part, stage_y[:1]), gather(down_part, stage_x[:1])
    chunks = [exchange(sent[0])]
    chunks += [exchange(after(value, (chunks[0], up_part, down_part))) for value in sent[1:]]
    solved = [attention(lows[0], starts[0], chunks[0])]

    up_bufs, up_place = in_order(gather_pair(up_part, stage_y[1:] + stage_x), places_a, direct)
    down_bufs, down_place = in_order(
        gather_pair(down_part, stage_x[1:] + stage_y), places_b, direct
    )
    half = jnp.stack([own_bit(*stage_x[-1]), own_bit(*stage_y[-1])]).astype(jnp.int32)
    up_send, up_keep, down_send, down_keep, mlp, norm2_grad, up_b_grad = feed_forward(
        units, half, after(norm2, (solved[0], chunks)), upstream, up_shift,
        up_bufs, up_place, down_bufs, down_place,
    )
    returned = [exchange(solved[0])]
    up_send, up_keep, down_send, down_keep = after(
        (up_send, up_keep, down_send, down_keep), returned[0]
    )
    part = returned[0]
    for q in range(1, seqs_each):
        chunk = after(chunks[q], (up_b_grad, returned[-1]))
        solved.append(attention(lows[q], starts[q], chunk))
        part = exchange(solved[q][:, : tokens // 4])
        rest = exchange(after(solved[q][:, tokens // 4 :], part))
        returned.append(jnp.concatenate([part, rest], axis=1))

    def halves(left, axis, bit, names):
        dim = names.index((axis, bit))
        span = left.shape[1] >> (dim + 1)
        mine_bit = own_bit(axis, bit)
        return [
            jnp.concatenate(
                [
                    lax.dynamic_slice_in_dim(left, 2 * at * span + index * span, span, 1)
                    for at in range(1 << dim)
                ],
                axis=1,
            )
            for index in (1 - mine_bit, mine_bit)
        ]

    bits = [("dp", bit) for bit in reversed(bits_of(dp)[1:])]
    bits += [("blk", bit) for bit in reversed(bits_of(blk))]
    bits += [("ulysses", bit) for bit in reversed(bits_of(ulysses))]
    low_z = list(reversed(stage_z))

    def names_of(with_core):
        return bits[: len(stage_x)] + [("dp", 1)] * with_core + bits[len(stage_x) :]

    class Reduction:
        def __init__(self, sent, total, order, with_core):
            self.names = names_of(with_core)
            self.order, self.with_core = order, with_core
            if sent is not None:
                self.names.remove(order[0])
                self.order = order[1:]
                total = total + swap(sent, *order[0]).astype(F32)
            units = total.shape[0] >> len(self.names)
            self.total = total.reshape((2,) * len(self.names) + (units, total.shape[1]))

        def step(self):
            axis, bit = self.order[0]
            dim = self.names.index((axis, bit))
            self.total = reduce_stage(self.total, dim, axis, bit)
            self.names.pop(dim)
            self.order = self.order[1:]

        def result(self):
            if self.with_core:
                return jnp.where(core == 0, self.total, self.total[::-1])
            return self.total

    def products(left, right, order, with_core):
        sent, kept = halves(left, *order[0], names_of(with_core))
        return dot(sent, right, TN).astype(BF16), kept, right

    xyz, yxz = stage_x[::-1] + stage_y[::-1] + low_z, stage_y[::-1] + stage_x[::-1] + low_z
    feed = [
        Reduction(down_send, down_keep, yxz, False),
        Reduction(up_send, up_keep, xyz, True),
    ]
    while len(feed[0].order) > len(low_z):
        for one in feed:
            one.total = after(one.total, part)
            one.step()
    for one in feed:
        one.total = after(one.total, returned[-1])
        while one.order:
            one.step()
    mixed, joined_grad = return_chunks(plan, cosine, sine, returned)
    cut = joined_grad.shape[1] // 2
    sent_a, *rest_a = products(norm1, joined_grad[:, :cut], xyz, True)
    sent_b, *rest_b = products(norm1, joined_grad[:, cut:], yxz, True)
    dense = Reduction(None, dot(mixed, upstream, TN), low_z + stage_x + stage_y, False)
    later = (sent_a, sent_b, dense.total)
    dense.step()
    grads_later, mixed_later, kept_a, kept_b = after(
        (joined_grad, mixed, rest_a[0], rest_b[0]), later
    )
    norm1_grad = dot(grads_later, qkv_full, NT)

    def columns_home(total, kinds):
        other = swap(total[1], "dp", 1)
        kept = total[0]
        pair = [jnp.where(core == 0, kept, other), jnp.where(core == 0, other, kept)]
        lead = kept.shape[0]
        if kinds == 1:
            pair = [value.reshape(lead, planes, ff // dp) for value in pair]
            return jnp.stack(pair, axis=2).reshape(lead, ff)
        inner = HEADS // dp // heads_each
        pair = [
            value.reshape(lead, planes, inner, 3, wide).transpose(0, 3, 1, 2, 4) for value in pair
        ]
        return jnp.stack(pair, axis=3).reshape(lead, 3 * width)

    branch = dot(mixed_later, dense_full) + mlp
    branch = branch[:half_rows] + swap(branch[half_rows:], "dp", 1)
    output = wide_inputs[:half_rows] + (branch + dense_shift + down_shift)
    output = output.astype(BF16).reshape(hidden.shape)
    slope = norm1_grad * gain_one + norm2_grad * gain_two
    slope = slope[:half_rows] + swap(slope[half_rows:], "dp", 1)
    own = normal[:half_rows]
    term = spread[:half_rows] * (
        slope
        - jnp.mean(slope, axis=-1, keepdims=True)
        - own * jnp.mean(slope * own, axis=-1, keepdims=True)
    )
    input_grad = (upstream[:half_rows].astype(F32) + term).astype(BF16).reshape(hidden.shape)

    def spread_core(value, kinds, last):
        value = value.reshape(kinds, planes, 1, last)
        empty = jnp.zeros_like(value)
        pair = [jnp.where(core == c, value, empty) for c in range(2)]
        return jnp.concatenate(pair, axis=2).reshape(-1)

    def total_of(value):
        return jnp.sum(value.astype(F32), axis=0)

    shift_grad = total_of(upstream[:half_rows])
    inner = HEADS // dp // heads_each
    qkv_b_grad = total_of(joined_grad).reshape(planes, inner, 3, wide).transpose(2, 0, 1, 3)
    qkv_b_grad = spread_core(qkv_b_grad, 3, inner * wide)
    small_grads = [
        total_of(norm1_grad * normal),
        total_of(norm1_grad),
        total_of(norm2_grad * normal),
        total_of(norm2_grad),
        qkv_b_grad,
        shift_grad,
        spread_core(up_b_grad, 1, ff // dp),
    ]
    small_sizes = [value.shape[0] // devices for value in small_grads]
    total = jnp.concatenate([value.reshape(devices, -1) for value in small_grads], axis=1)
    total = jnp.pad(total, ((0, 0), (0, -total.shape[1] % 128)))
    total = total.reshape((2,) * (len(bits) + 1) + (1, -1))

    last = [
        Reduction(sent_a, dot(kept_a, rest_a[1], TN), xyz, True),
        Reduction(sent_b, dot(kept_b, rest_b[1], TN), yxz, True),
        dense,
    ]
    names = names_of(True)
    done = (output, input_grad)
    for axis, bit in xyz + [("dp", 1)]:
        dim = names.index((axis, bit))
        names.pop(dim)
        if last[0].order:
            held = [one.total for one in last]
            if len(last[0].order) == 1:
                held = after(held, done)
            held, total = lax.optimization_barrier((held, total))
            for one, value in zip(last, held):
                one.total = value
                if one.order:
                    one.step()
        total = reduce_stage(total, dim, axis, bit, F32)
    qkv_a, qkv_b, dense_w_grad = [one.result() for one in last]
    down_w_grad, up_w_grad = [one.result() for one in feed]
    up_w_grad = columns_home(up_w_grad, 1)
    qkv_w_grad = columns_home(jnp.concatenate([qkv_a, qkv_b], axis=-1), 3)
    total = total.reshape(-1)
    smalls, at = [], 0
    for size in small_sizes:
        smalls.append(total[at : at + size])
        at += size
    return (
        output,
        input_grad,
        smalls[0],
        smalls[1],
        smalls[2],
        smalls[3],
        qkv_w_grad,
        smalls[4],
        dense_w_grad,
        smalls[5],
        up_w_grad,
        smalls[6],
        down_w_grad,
        smalls[5],
    )


def solution(mesh):
    rows = ("dp", "blk", "ulysses")
    tokens = P("dp", ("blk", "ulysses"), None)
    vector, matrix = P(rows), P(rows, None)
    in_specs = (tokens, P("dp", "blk")) + (vector,) * 4 + (matrix, vector) * 4 + (tokens,)
    out_specs = (tokens, tokens) + (vector,) * 4 + (matrix, vector) * 4
    return jax.shard_map(
        on_device, mesh=mesh, in_specs=in_specs, out_specs=out_specs, check_vma=False
    )
```

```python
from functools import partial

import jax
import jax.numpy as jnp
from jax import lax
from jax.experimental import pallas as pl
from jax.experimental.pallas import tpu as pltpu
from jax.sharding import PartitionSpec as P

HEADS = 16
HEAD_DIM = 64
ROT = 16
EPSILON = 1e-05
MASKED_SCORE = -1e30
LOG2_E = 1.4426950408889634
RANKS = ("blk", "ulysses")
F32 = jnp.float32
BF16 = jnp.bfloat16
NN = (((1,), (0,)), ((), ()))
NT = (((1,), (1,)), ((), ()))
TN = (((0,), (0,)), ((), ()))
ANY = pl.BlockSpec(memory_space=pl.ANY)
VMEM = pl.BlockSpec(memory_space=pltpu.VMEM)
SMEM = pl.BlockSpec(memory_space=pltpu.SMEM)


def dot(left, right, dims=NN):
    return lax.dot_general(left, right, dims, preferred_element_type=F32)


def swap(value, axis, bit):
    size = lax.axis_size(axis)
    return lax.ppermute(value, axis, [(i, i ^ bit) for i in range(size)])


def bits_of(size):
    return [1 << k for k in range(size.bit_length() - 1)]


def gather(value, stages):
    for axis, bit in stages:
        value = jnp.concatenate([value, swap(value, axis, bit)], axis=0)
    return value


def after(value, other):
    return lax.optimization_barrier((value, other))[0]


def gather_pair(value, stages):
    value = gather(value, stages[:-1])
    return [value, swap(value, *stages[-1])]


def natural_weight(axis, bit):
    ulysses = lax.axis_size("ulysses")
    if axis == "ulysses":
        return bit
    if axis == "blk":
        return bit * ulysses
    return (bit // 2) * ulysses * lax.axis_size("blk")


def places_of(stages, mine):
    slot = jnp.arange(1 << len(stages), dtype=jnp.int32)
    relative = jnp.zeros_like(slot)
    for at, (axis, bit) in enumerate(stages):
        relative = relative + ((slot >> at) % 2) * natural_weight(axis, bit)
    return relative ^ mine


def own_bit(axis, bit):
    return (lax.axis_index(axis) // bit) % 2


def pick(value, index, dim):
    return lax.dynamic_index_in_dim(value, index, dim, keepdims=False)


def reduce_stage(total, dim, axis, bit, wire=BF16):
    mine = own_bit(axis, bit)
    sent = pick(total, 1 - mine, dim).astype(wire)
    return pick(total, mine, dim) + swap(sent, axis, bit).astype(F32)


def params(mib):
    return pltpu.CompilerParams(vmem_limit_bytes=mib << 20)


class Sems:
    def __init__(self, array):
        self.array, self.used = array, 0

    def copy(self, source, target):
        self.used += 1
        return pltpu.make_async_copy(source, target, self.array.at[self.used - 1])


def run(copies):
    for copy in copies:
        copy.start()
    for copy in copies:
        copy.wait()


def slot_refs(refs):
    return [ref.at[at] for ref in refs for at in range(ref.shape[0])]


def in_order(buffers, places, direct):
    if direct:
        return buffers, places
    natural = jnp.arange(places.shape[0], dtype=jnp.int32)
    whole = jnp.concatenate(buffers, axis=0)
    return [jnp.take(whole, jnp.argsort(places), axis=0)], natural


def rotate(value, cosine, sine, sign):
    lane = lax.broadcasted_iota(jnp.int32, value.shape, 1) % HEAD_DIM
    lanes = value.shape[1]
    other = jnp.where(
        lane < ROT // 2,
        pltpu.roll(value, lanes - ROT // 2, 1),
        pltpu.roll(value, ROT // 2, 1),
    )
    return value * cosine + other * (sine * sign)


def first_kernel(plan, places, counts, place_a, place_b, *rest):
    ranks, seqs, per_rank, tokens, wide = plan
    planes, inner, piece = places
    x_ref, cot_ref, bias_ref, cos_ref, sin_ref = rest[:5]
    a_refs, b_refs = rest[5 : 5 + counts[0]], rest[5 + counts[0] : 5 + sum(counts)]
    rest = rest[5 + sum(counts) :]
    out_refs, (w_ref, dense_ref, in_sems) = rest[:per_rank], rest[per_rank:]
    seq_groups = seqs // per_rank
    groups = ranks // seq_groups
    width = x_ref.shape[1]
    half = width // 2
    give = Sems(in_sems)
    copies = []
    for slots, place_ref, second in ((a_refs, place_a, False), (b_refs, place_b, True)):
        for at, slot in enumerate(slot_refs(slots)):
            place = place_ref[at]
            for part in range(2):
                source = slot.at[pl.ds(part * piece, piece)]
                row = ((place // inner) * 2 + part) * inner + place % inner
                span = pl.ds(pl.multiple_of(row * piece, piece), piece)
                if second:
                    own = pl.ds(pl.multiple_of(place * piece, piece), piece)
                    copies.append(
                        give.copy(source.at[:, pl.ds(0, half)], w_ref.at[span, pl.ds(width, half)])
                    )
                    copies.append(
                        give.copy(
                            source.at[:, pl.ds(half, half)],
                            dense_ref.at[own, pl.ds(part * half, half)],
                        )
                    )
                else:
                    copies.append(give.copy(source, w_ref.at[span, pl.ds(0, width)]))
    run(copies)

    for q in range(per_rank):
        held = out_refs[q]

        def step(group, carry):
            rows = pl.ds(pl.multiple_of((group * per_rank + q) * tokens, tokens), tokens)
            x = x_ref[rows, :]
            cosine, sine = cos_ref[rows, :], sin_ref[rows, :]
            grads = dot(cot_ref[rows, :], dense_ref[...], NT).astype(BF16)
            for g in range(groups):
                cols = slice(3 * g * wide, 3 * (g + 1) * wide)
                joined = dot(x, w_ref[:, cols]) + bias_ref[:, cols]
                turned = rotate(joined[:, : 2 * wide], cosine, sine, 1.0)
                rank = g * seq_groups + group
                held[rank, :, : 2 * wide] = turned.astype(BF16)
                held[rank, :, 2 * wide : 3 * wide] = joined[:, 2 * wide :].astype(BF16)
                held[rank, :, 3 * wide :] = grads[:, g * wide : (g + 1) * wide]
            return carry

        lax.fori_loop(0, seq_groups, step, 0)


def first_chunks(plan, places, a, b, place_a, place_b, x, cot, bias, cosine, sine):
    ranks, seqs, per_rank, tokens, wide = plan
    width = x.shape[1]
    slots = place_a.shape[0]
    outs = pl.pallas_call(
        partial(first_kernel, plan, places, (len(a), len(b))),
        in_specs=[SMEM] * 2 + [VMEM] * 5 + [ANY] * (len(a) + len(b)),
        out_specs=[VMEM] * (per_rank + 2),
        out_shape=[jax.ShapeDtypeStruct((ranks, tokens, 4 * wide), BF16)] * per_rank
        + [
            jax.ShapeDtypeStruct((width, 3 * width // 2), BF16),
            jax.ShapeDtypeStruct((width // 2, width), BF16),
        ],
        scratch_shapes=[pltpu.SemaphoreType.DMA((6 * slots,))],
        compiler_params=params(48),
        cost_estimate=pl.CostEstimate(
            flops=4 * x.shape[0] * width * width, bytes_accessed=20 << 20, transcendentals=0
        ),
        name="first_chunks",
    )(place_a, place_b, x, cot, bias, cosine, sine, *a, *b)
    return outs[:per_rank], outs[per_rank], outs[per_rank + 1]


def feed_kernel(places, counts, block, side_unit, up_place, down_place, half_ref, x_ref, cot_ref, bias_ref, *rest):
    planes, inner, piece = places
    up_refs, down_refs = rest[: counts[0]], rest[counts[0] : sum(counts)]
    rest = rest[sum(counts) :]
    up_send, up_keep, down_send, down_keep, out_ref, norm_ref, sum_ref = rest[:7]
    up_w, down_w, act, grad, up_s, up_k, down_s, down_k, in_sems, sems = rest[7:]
    rows, width = x_ref.shape
    ff = down_w.shape[0]
    blocks = ff // block
    tile = rows // 2
    give = Sems(in_sems)
    copies = []
    for at, slot in enumerate(slot_refs(up_refs)):
        place = up_place[at]
        for part in range(2):
            row = ((place // inner) * 2 + part) * inner + place % inner
            span = pl.ds(pl.multiple_of(row * piece, piece), piece)
            copies.append(give.copy(slot.at[pl.ds(part * piece, piece)], up_w.at[span]))
    unit = down_refs[0].shape[1]
    for at, slot in enumerate(slot_refs(down_refs)):
        span = pl.ds(pl.multiple_of(down_place[at] * unit, unit), unit)
        copies.append(give.copy(slot, down_w.at[span]))
    run(copies)
    mine, mine_block = half_ref[0], half_ref[1]
    span_half = pl.ds(pl.multiple_of(mine * (width // 2), width // 2), width // 2)
    span_other = pl.ds(pl.multiple_of((1 - mine) * (width // 2), width // 2), width // 2)

    def out_copies(step):
        cols = pl.ds(pl.multiple_of(natural(step) * block, block), block)
        at = step % (blocks // 2)
        span = pl.ds(pl.multiple_of(at * block, block), block)
        return [
            pltpu.make_async_copy(up_s.at[step], up_send.at[:, cols], sems.at[0, step]),
            pltpu.make_async_copy(up_k.at[step], up_keep.at[:, cols], sems.at[1, step]),
        ], span

    def natural(step):
        side = jnp.where(step < blocks // 2, 1 - mine_block, mine_block)
        at = step % (blocks // 2)
        return ((at // side_unit) * 2 + side) * side_unit + at % side_unit

    def one(step, carry):
        at = natural(step)
        cols = pl.ds(pl.multiple_of(at * block, block), block)
        up_b = up_w[:, cols]
        down_b = down_w[cols, :]
        bias = bias_ref[:, cols]
        for r in range(2):
            span = slice(r * tile, (r + 1) * tile)
            pre = dot(x_ref[span, :], up_b) + bias
            cdf = 0.5 * (1.0 + lax.erf(pre * (0.5**0.5)))
            slope = cdf + pre * (jnp.exp2(pre * pre * (-0.5 * LOG2_E)) * 0.3989422804014327)
            active = (pre * cdf).astype(BF16)
            act[span, :] = active
            back = (dot(cot_ref[span, :], down_b, NT) * slope).astype(BF16)
            grad[span, :] = back
            out = dot(active, down_b)
            norm = dot(back, up_b, NT)

            @pl.when(step == 0)
            def _():
                out_ref[span, :] = out
                norm_ref[span, :] = norm

            @pl.when(step > 0)
            def _():
                out_ref[span, :] += out
                norm_ref[span, :] += norm

        sum_ref[:, cols] = jnp.sum(grad[...].astype(F32), axis=0, keepdims=True)
        up_g = dot(x_ref[:, span_other], grad[...], TN)
        up_s[step] = up_g.astype(BF16)
        up_k[step] = dot(x_ref[:, span_half], grad[...], TN)
        pair, span = out_copies(step)
        for copy in pair:
            copy.start()
        down_g = dot(act[...], cot_ref[...], TN)

        @pl.when(step < blocks // 2)
        def _():
            down_s[step] = down_g.astype(BF16)
            pltpu.make_async_copy(down_s.at[step], down_send.at[span], sems.at[2, step]).start()

        @pl.when(step >= blocks // 2)
        def _():
            here = step - blocks // 2
            down_k[here] = down_g
            pltpu.make_async_copy(down_k.at[here], down_keep.at[span], sems.at[2, step]).start()

        return carry

    lax.fori_loop(0, blocks, one, 0)
    for step in range(blocks):
        pair, span = out_copies(step)
        for copy in pair:
            copy.wait()
        if step < blocks // 2:
            pltpu.make_async_copy(down_s.at[step], down_send.at[span], sems.at[2, step]).wait()
        else:
            here = step - blocks // 2
            pltpu.make_async_copy(down_k.at[here], down_keep.at[span], sems.at[2, step]).wait()


def feed_forward(places, half, x, cot, bias, up, up_place, down, down_place):
    rows, width = x.shape
    ff = bias.shape[1]
    block = min(256, ff // 2)
    blocks = ff // block
    return pl.pallas_call(
        partial(feed_kernel, places, (len(up), len(down)), block, blocks // (2 * places[0])),
        in_specs=[SMEM] * 3 + [VMEM] * 3 + [ANY] * (len(up) + len(down)),
        out_specs=[ANY] * 4 + [VMEM] * 3,
        out_shape=[
            jax.ShapeDtypeStruct((width // 2, ff), BF16),
            jax.ShapeDtypeStruct((width // 2, ff), F32),
            jax.ShapeDtypeStruct((ff // 2, width), BF16),
            jax.ShapeDtypeStruct((ff // 2, width), F32),
            jax.ShapeDtypeStruct((rows, width), F32),
            jax.ShapeDtypeStruct((rows, width), F32),
            jax.ShapeDtypeStruct((1, ff), F32),
        ],
        scratch_shapes=[
            pltpu.VMEM((width, ff), BF16),
            pltpu.VMEM((ff, width), BF16),
            pltpu.VMEM((rows, block), BF16),
            pltpu.VMEM((rows, block), BF16),
            pltpu.VMEM((blocks, width // 2, block), BF16),
            pltpu.VMEM((blocks, width // 2, block), F32),
            pltpu.VMEM((blocks // 2, block, width), BF16),
            pltpu.VMEM((blocks // 2, block, width), F32),
            pltpu.SemaphoreType.DMA((2 * up_place.shape[0] + down_place.shape[0],)),
            pltpu.SemaphoreType.DMA((3, blocks)),
        ],
        compiler_params=params(58),
        cost_estimate=pl.CostEstimate(
            flops=12 * rows * width * ff, bytes_accessed=32 << 20, transcendentals=2 * rows * ff
        ),
        name="feed_forward",
    )(up_place, down_place, half, x, cot, bias, *up, *down)


def attention_kernel(low_ref, start_ref, chunk, *rest):
    outs, turned, natural, scores, products, sums = rest
    ranks, block, wide = chunk.shape[0], chunk.shape[1], chunk.shape[2] // 4
    heads = wide // HEAD_DIM
    scale = HEAD_DIM ** (-0.5)
    power = scale * LOG2_E
    def prepare(b, carry):
        kinds = chunk[b]
        turned[b] = kinds.T
        for h in range(heads):
            own = slice(h * HEAD_DIM, (h + 1) * HEAD_DIM)
            for kind in range(4):
                natural[h, kind, b] = kinds[:, kind * wide : (kind + 1) * wide][:, own]
            sums[h, 0, b] = jnp.zeros((block, HEAD_DIM), F32)
            sums[h, 1, b] = jnp.zeros((block, HEAD_DIM), F32)
        return carry

    lax.fori_loop(0, ranks, prepare, 0)

    def rows_of(h, kind):
        return slice(kind * wide + h * HEAD_DIM, kind * wide + (h + 1) * HEAD_DIM)

    def queries(i, carry):
        start = start_ref[i]
        query = i * block + lax.broadcasted_iota(jnp.int32, (1, block), 1)
        low = low_ref[i]

        first, last = low // 2, (i + 2) // 2

        def score(pair, tops):
            for j in (2 * pair, 2 * pair + 1):
                key = j * block + lax.broadcasted_iota(jnp.int32, (block, block), 0)
                allowed = (key <= query) & (key >= start)
                found = []
                for h in range(heads):
                    value = dot(natural[h, 1, j], turned[i, rows_of(h, 0), :])
                    value = jnp.where(allowed, value, MASKED_SCORE)
                    scores[h, j] = value
                    found.append(jnp.maximum(tops[h], jnp.max(value, axis=0, keepdims=True)))
                tops = tuple(found)
            return tops

        tops = lax.fori_loop(first, last, score, (jnp.full((1, block), MASKED_SCORE, F32),) * heads)

        def weigh(pair, carried):
            for j in (2 * pair, 2 * pair + 1):
                found = []
                for h in range(heads):
                    total, delta = carried[h]
                    expo = jnp.exp2((scores[h, j] - tops[h]) * power)
                    scores[h, j] = expo
                    product = dot(natural[h, 2, j], turned[i, rows_of(h, 3), :])
                    products[h, j] = product
                    found.append(
                        (
                            total + jnp.sum(expo, axis=0, keepdims=True),
                            delta + jnp.sum(expo * product, axis=0, keepdims=True),
                        )
                    )
                carried = tuple(found)
            return carried

        zero = jnp.zeros((1, block), F32)
        stats = lax.fori_loop(first, last, weigh, ((zero, zero),) * heads)
        inverse = [1.0 / total for total, _ in stats]
        deltas = [delta * inv for (_, delta), inv in zip(stats, inverse)]

        def collect(pair, carried):
            for j in (2 * pair, 2 * pair + 1):
                found = []
                for h in range(heads):
                    mixed, query_grad = carried[h]
                    prob = scores[h, j] * inverse[h]
                    rounded = prob.astype(BF16)
                    slope = (prob * (products[h, j] - deltas[h])).astype(BF16)
                    mixed = mixed + dot(turned[j, rows_of(h, 2), :], rounded)
                    query_grad = query_grad + dot(turned[j, rows_of(h, 1), :], slope)
                    sums[h, 0, j] += dot(slope, natural[h, 0, i])
                    sums[h, 1, j] += dot(rounded, natural[h, 3, i])
                    found.append((mixed, query_grad))
                carried = tuple(found)
            return carried

        empty = jnp.zeros((HEAD_DIM, block), F32)
        totals = lax.fori_loop(first, last, collect, ((empty, empty),) * heads)
        mixed = jnp.concatenate([t[0] for t in totals], axis=0)
        query_grad = jnp.concatenate([t[1] for t in totals], axis=0)
        outs[i, :, :wide] = mixed.T.astype(BF16)
        outs[i, :, wide : 2 * wide] = (query_grad * scale).T.astype(BF16)
        return carry

    lax.fori_loop(0, ranks, queries, 0)

    def finish(b, carry):
        for kind in range(2):
            value = jnp.concatenate([sums[h, kind, b] for h in range(heads)], axis=1)
            if kind == 0:
                value = value * scale
            outs[b, :, (2 + kind) * wide : (3 + kind) * wide] = value.astype(BF16)
        return carry

    lax.fori_loop(0, ranks, finish, 0)


def attention(low, start, chunk):
    ranks, block, wide = chunk.shape[0], chunk.shape[1], chunk.shape[2] // 4
    heads = wide // HEAD_DIM
    pairs = ranks * (ranks + 1) // 2 * block * block * heads
    return pl.pallas_call(
        attention_kernel,
        in_specs=[SMEM, VMEM, VMEM],
        out_specs=VMEM,
        out_shape=jax.ShapeDtypeStruct(chunk.shape, BF16),
        scratch_shapes=[
            pltpu.VMEM((ranks, 4 * wide, block), BF16),
            pltpu.VMEM((heads, 4, ranks, block, HEAD_DIM), BF16),
            pltpu.VMEM((heads, ranks, block, block), F32),
            pltpu.VMEM((heads, ranks, block, block), F32),
            pltpu.VMEM((heads, 2, ranks, block, HEAD_DIM), F32),
        ],
        compiler_params=params(56),
        cost_estimate=pl.CostEstimate(
            flops=2 * 6 * 4 * HEAD_DIM * pairs,
            bytes_accessed=8 * ranks * block * wide * 2,
            transcendentals=pairs,
        ),
        name="attention",
    )(low, start, chunk)


def return_kernel(plan, cos_ref, sin_ref, *rest):
    ranks, seqs, per_rank, tokens, wide = plan
    in_refs, (mixed_ref, grad_ref) = rest[:per_rank], rest[per_rank:]
    seq_groups = seqs // per_rank
    groups = ranks // seq_groups
    for q in range(per_rank):
        held = in_refs[q]

        def step(group, carry):
            rows = pl.ds(pl.multiple_of((group * per_rank + q) * tokens, tokens), tokens)
            cosine, sine = cos_ref[rows, :], sin_ref[rows, :]
            for g in range(groups):
                value = held[g * seq_groups + group]
                mixed_ref[rows, g * wide : (g + 1) * wide] = value[:, :wide]
                turned = rotate(value[:, wide : 3 * wide].astype(F32), cosine, sine, -1.0)
                at = 3 * g * wide
                grad_ref[rows, at : at + 2 * wide] = turned.astype(BF16)
                grad_ref[rows, at + 2 * wide : at + 3 * wide] = value[:, 3 * wide :]
            return carry

        lax.fori_loop(0, seq_groups, step, 0)


def return_chunks(plan, cosine, sine, chunks):
    ranks, seqs, per_rank, tokens, wide = plan
    groups = ranks * per_rank // seqs
    return pl.pallas_call(
        partial(return_kernel, plan),
        in_specs=[VMEM] * (2 + per_rank),
        out_specs=[VMEM, VMEM],
        out_shape=[
            jax.ShapeDtypeStruct((seqs * tokens, groups * wide), BF16),
            jax.ShapeDtypeStruct((seqs * tokens, 3 * groups * wide), BF16),
        ],
        compiler_params=params(40),
        cost_estimate=pl.CostEstimate(
            flops=8 * seqs * tokens * 4 * groups * wide, bytes_accessed=12 << 20, transcendentals=0
        ),
        name="return_chunks",
    )(cosine, sine, *chunks)


def on_device(
    hidden,
    positions,
    ln1_gain,
    ln1_bias,
    ln2_gain,
    ln2_bias,
    qkv_weight,
    qkv_bias,
    dense_weight,
    dense_bias,
    up_weight,
    up_bias,
    down_weight,
    down_bias,
    cotangent,
):
    seq_dp, tokens, width = hidden.shape
    ulysses, blk, dp = lax.axis_size("ulysses"), lax.axis_size("blk"), lax.axis_size("dp")
    planes = dp // 2
    ranks = blk * ulysses
    core = lax.axis_index("dp") % 2
    rank = lax.axis_index("blk") * ulysses + lax.axis_index("ulysses")
    mine = (lax.axis_index("dp") // 2) * ranks + rank
    devices = dp * ranks
    half_rows = seq_dp * tokens
    rows = 2 * half_rows
    piece = width // devices
    ff = up_weight.shape[1]

    seqs = 2 * seq_dp
    pairs = seqs * (HEADS // 2) // ranks
    heads_each = 2 if pairs % 2 == 0 else 1
    seqs_each = pairs // heads_each
    seq_groups = seqs // seqs_each
    groups = HEADS // 2 // heads_each
    wide = heads_each * HEAD_DIM

    def with_partner(value):
        return jnp.concatenate([value, swap(value, "dp", 1)], axis=0)

    stage_z = [("ulysses", bit) for bit in reversed(bits_of(ulysses))]
    stage_y = [("blk", bit) for bit in bits_of(blk)]
    stage_x = [("dp", bit) for bit in bits_of(dp)[1:]]
    order_a, order_b = stage_z + stage_y + stage_x, stage_z + stage_x + stage_y

    def core_columns(value, lead, index):
        value = value.reshape(lead, 3, planes, 2, HEADS // dp // heads_each, wide)
        value = pick(value, index, 3)
        return value.transpose(0, 2, 3, 1, 4).reshape(lead, 3 * width // 2)

    def core_ff(value, lead, index):
        return pick(value.reshape(lead, planes, 2, ff // dp), index, 2).reshape(lead, ff // 2)

    def both_cores(kept, sent):
        came = swap(sent, "dp", 1)
        return jnp.concatenate(
            [jnp.where(core == 0, kept, came), jnp.where(core == 0, came, kept)], axis=0
        )

    qkv_piece = both_cores(
        core_columns(qkv_weight, piece, core), core_columns(qkv_weight, piece, 1 - core)
    )
    dense_piece = jnp.concatenate(
        [dense_weight[:, : width // 2], dense_weight[:, width // 2 :]], axis=0
    )
    first = jnp.concatenate([qkv_piece, dense_piece], axis=1)[None]
    small = [ln1_gain, ln1_bias, ln2_gain, ln2_bias, qkv_bias, dense_bias, up_bias, down_bias]
    sizes = [value.shape[0] for value in small]
    length = sum(sizes)
    padded = -(-length // 128) * 128
    packed = jnp.concatenate(small + [jnp.zeros((padded - length,), BF16)])[None]
    places = with_partner(positions)
    every = gather(places[None], stage_y)
    up_piece = both_cores(core_ff(up_weight, piece, core), core_ff(up_weight, piece, 1 - core))
    up_part, down_part = up_piece[None], down_weight[None]

    packed = gather(packed, [("dp", 1)])
    beside = stage_x + stage_y
    for at, stage in enumerate(stage_z):
        packed = gather(after(packed, (first, every)), beside[at : at + 1])
        first = gather(first, [stage])
        if at == 0:
            up_part, down_part = after((up_part, down_part), first)
    up_part, down_part = gather(up_part, stage_z[:1]), gather(down_part, stage_z[:1])
    packed = gather(after(packed, first), beside[len(stage_z) :] + stage_z[:1])

    direct = piece % 16 == 0
    units = (planes, ranks, piece)
    places_a, places_b = places_of(order_a, mine), places_of(order_b, mine)
    first_a = gather_pair(first[..., :width], stage_y + stage_x)
    first_b = gather_pair(first[..., width:], stage_x + stage_y)
    packed = gather(after(packed, (first_a[0], first_b[0])), stage_z[1:])
    up_part, down_part = after((up_part, down_part), (packed, first_a[0], first_b[0]))
    up_part, down_part = gather(up_part, stage_z[1:]), gather(down_part, stage_z[1:])
    early = (up_part, down_part)
    first_a, place_a = in_order(first_a, places_a, direct)
    first_b, place_b = in_order(first_b, places_b, direct)

    relative = jnp.zeros((devices,), jnp.int32)
    weights = [ranks] + [
        natural_weight(axis, bit) * (2 if axis == "dp" else 1)
        for axis, bit in beside + stage_z
    ]
    for at, weight in enumerate(weights):
        relative = relative + ((jnp.arange(devices, dtype=jnp.int32) >> at) % 2) * weight
    home = (lax.axis_index("dp") * ranks + rank) ^ relative
    sorting = (jnp.arange(devices, dtype=jnp.int32)[:, None] == home[None, :]).astype(BF16)
    packed = dot(sorting, packed)
    vectors, at = [], 0
    for size in sizes:
        vectors.append(packed[:, at : at + size].reshape(-1))
        at += size
    gain_one, bias_one, gain_two, bias_two, qkv_shift, dense_shift, up_shift, down_shift = vectors
    qkv_shift = core_columns(qkv_shift, 1, core)
    up_shift = core_ff(up_shift, 1, core)

    inputs = with_partner(hidden.reshape(half_rows, width))
    upstream = with_partner(cotangent.reshape(half_rows, width))
    wide_inputs = inputs.astype(F32)
    center = wide_inputs - jnp.mean(wide_inputs, axis=-1, keepdims=True)
    spread = lax.rsqrt(jnp.mean(center * center, axis=-1, keepdims=True) + EPSILON)
    normal = center * spread
    norm1 = (normal * gain_one + bias_one).astype(BF16)
    norm2 = (normal * gain_two + bias_two).astype(BF16)

    own_places = lax.dynamic_slice_in_dim(
        places, lax.axis_index("ulysses") * tokens, tokens, 1
    ).reshape(rows, 1)
    lane = jnp.arange(2 * wide, dtype=jnp.int32) % HEAD_DIM
    freqs = 10000.0 ** (-((lane % (ROT // 2)).astype(F32) * 2.0 / ROT))
    freqs = jnp.where(lane < ROT, freqs, 0.0)
    angles = own_places.astype(F32) * freqs
    cosine = jnp.cos(angles)
    sine = jnp.sin(angles) * jnp.where(lane < ROT // 2, -1.0, 1.0)

    here = lax.axis_index("blk")
    every = jnp.stack([pick(every, here ^ j, 0) for j in range(blk)], axis=1)
    every = every.reshape(seqs, ranks * tokens)
    starts = jnp.arange(ranks * tokens, dtype=jnp.int32) - every
    starts = pick(starts.reshape(seq_groups, seqs_each, ranks, 1, tokens), rank % seq_groups, 0)
    lows = starts[:, :, 0, 0] // tokens

    def exchange(chunks):
        return lax.all_to_all(chunks, RANKS, split_axis=0, concat_axis=0, tiled=True)

    plan = (ranks, seqs, seqs_each, tokens, wide)
    sent, qkv_full, dense_full = first_chunks(
        plan, units, first_a, first_b, place_a, place_b,
        after(norm1, early), upstream, qkv_shift, cosine, sine,
    )
    up_part, down_part = gather(up_part, stage_y[:1]), gather(down_part, stage_x[:1])
    chunks = [exchange(sent[0])]
    chunks += [exchange(after(value, (chunks[0], up_part, down_part))) for value in sent[1:]]
    solved = [attention(lows[0], starts[0], chunks[0])]

    up_bufs, up_place = in_order(gather_pair(up_part, stage_y[1:] + stage_x), places_a, direct)
    down_bufs, down_place = in_order(
        gather_pair(down_part, stage_x[1:] + stage_y), places_b, direct
    )
    half = jnp.stack([own_bit(*stage_x[-1]), own_bit(*stage_y[-1])]).astype(jnp.int32)
    up_send, up_keep, down_send, down_keep, mlp, norm2_grad, up_b_grad = feed_forward(
        units, half, after(norm2, (solved[0], chunks)), upstream, up_shift,
        up_bufs, up_place, down_bufs, down_place,
    )
    returned = [exchange(solved[0])]
    up_send, up_keep, down_send, down_keep = after(
        (up_send, up_keep, down_send, down_keep), returned[0]
    )
    part = returned[0]
    for q in range(1, seqs_each):
        chunk = after(chunks[q], (up_b_grad, returned[-1]))
        solved.append(attention(lows[q], starts[q], chunk))
        part = exchange(solved[q][:, : tokens // 4])
        rest = exchange(after(solved[q][:, tokens // 4 :], part))
        returned.append(jnp.concatenate([part, rest], axis=1))

    def halves(left, axis, bit, names):
        dim = names.index((axis, bit))
        span = left.shape[1] >> (dim + 1)
        mine_bit = own_bit(axis, bit)
        return [
            jnp.concatenate(
                [
                    lax.dynamic_slice_in_dim(left, 2 * at * span + index * span, span, 1)
                    for at in range(1 << dim)
                ],
                axis=1,
            )
            for index in (1 - mine_bit, mine_bit)
        ]

    bits = [("dp", bit) for bit in reversed(bits_of(dp)[1:])]
    bits += [("blk", bit) for bit in reversed(bits_of(blk))]
    bits += [("ulysses", bit) for bit in reversed(bits_of(ulysses))]
    low_z = list(reversed(stage_z))

    def names_of(with_core):
        return bits[: len(stage_x)] + [("dp", 1)] * with_core + bits[len(stage_x) :]

    class Reduction:
        def __init__(self, sent, total, order, with_core):
            self.names = names_of(with_core)
            self.order, self.with_core = order, with_core
            if sent is not None:
                self.names.remove(order[0])
                self.order = order[1:]
                total = total + swap(sent, *order[0]).astype(F32)
            units = total.shape[0] >> len(self.names)
            self.total = total.reshape((2,) * len(self.names) + (units, total.shape[1]))

        def pop(self):
            axis, bit = self.order[0]
            dim = self.names.index((axis, bit))
            self.names.pop(dim)
            self.order = self.order[1:]
            return dim, axis, bit

        def step(self):
            dim, axis, bit = self.pop()
            self.total = reduce_stage(self.total, dim, axis, bit)

        def result(self):
            if self.with_core:
                return jnp.where(core == 0, self.total, self.total[::-1])
            return self.total

    def step_together(reductions):
        sent, kept = [], []
        for one in reductions:
            dim, axis, bit = one.pop()
            mine_bit = own_bit(axis, bit)
            part = pick(one.total, 1 - mine_bit, dim).astype(BF16)
            cols = part.reshape(-1, part.shape[-1])
            sent += [cols[:, at : at + width] for at in range(0, cols.shape[1], width)]
            kept.append(pick(one.total, mine_bit, dim))
        came = swap(jnp.concatenate(sent, axis=0), axis, bit).astype(F32)
        at = 0
        for one, keep in zip(reductions, kept):
            count = keep.shape[-1] // width
            rows_each = keep.size // keep.shape[-1]
            cols = [came[at + k * rows_each : at + (k + 1) * rows_each] for k in range(count)]
            at += count * rows_each
            one.total = keep + jnp.concatenate(cols, axis=1).reshape(keep.shape)

    def products(left, right, order, with_core):
        sent, kept = halves(left, *order[0], names_of(with_core))
        return dot(sent, right, TN).astype(BF16), kept, right

    xyz, yxz = stage_x[::-1] + stage_y[::-1] + low_z, stage_y[::-1] + stage_x[::-1] + low_z
    feed = [
        Reduction(down_send, down_keep, yxz, False),
        Reduction(up_send, up_keep, xyz, True),
    ]
    while len(feed[0].order) > len(low_z):
        for one in feed:
            one.total = after(one.total, part)
            one.step()
    for one, value in zip(feed, after([one.total for one in feed], returned[-1])):
        one.total = value
    while feed[0].order:
        step_together(feed)
    mixed, joined_grad = return_chunks(plan, cosine, sine, returned)
    cut = joined_grad.shape[1] // 2
    sent_a, *rest_a = products(norm1, joined_grad[:, :cut], xyz, True)
    sent_b, *rest_b = products(norm1, joined_grad[:, cut:], yxz, True)
    dense = Reduction(None, dot(mixed, upstream, TN), low_z + stage_x + stage_y, False)
    later = (sent_a, sent_b, dense.total)
    dense.step()
    grads_later, mixed_later, kept_a, kept_b = after(
        (joined_grad, mixed, rest_a[0], rest_b[0]), later
    )
    norm1_grad = dot(grads_later, qkv_full, NT)

    def columns_home(total, kinds):
        other = swap(total[1], "dp", 1)
        kept = total[0]
        pair = [jnp.where(core == 0, kept, other), jnp.where(core == 0, other, kept)]
        lead = kept.shape[0]
        if kinds == 1:
            pair = [value.reshape(lead, planes, ff // dp) for value in pair]
            return jnp.stack(pair, axis=2).reshape(lead, ff)
        inner = HEADS // dp // heads_each
        pair = [
            value.reshape(lead, planes, inner, 3, wide).transpose(0, 3, 1, 2, 4) for value in pair
        ]
        return jnp.stack(pair, axis=3).reshape(lead, 3 * width)

    branch = dot(mixed_later, dense_full) + mlp
    slope = norm1_grad * gain_one + norm2_grad * gain_two

    def finish(branch, slope, branch_came, slope_came):
        branch = branch[:half_rows] + branch_came
        output = wide_inputs[:half_rows] + (branch + dense_shift + down_shift)
        output = output.astype(BF16).reshape(hidden.shape)
        slope = slope[:half_rows] + slope_came
        own = normal[:half_rows]
        term = spread[:half_rows] * (
            slope
            - jnp.mean(slope, axis=-1, keepdims=True)
            - own * jnp.mean(slope * own, axis=-1, keepdims=True)
        )
        input_grad = upstream[:half_rows].astype(F32) + term
        return output, input_grad.astype(BF16).reshape(hidden.shape)

    def spread_core(value, kinds, last):
        value = value.reshape(kinds, planes, 1, last)
        empty = jnp.zeros_like(value)
        pair = [jnp.where(core == c, value, empty) for c in range(2)]
        return jnp.concatenate(pair, axis=2).reshape(-1)

    def total_of(value):
        return jnp.sum(value.astype(F32), axis=0)

    shift_grad = total_of(upstream[:half_rows])
    inner = HEADS // dp // heads_each
    qkv_b_grad = total_of(joined_grad).reshape(planes, inner, 3, wide).transpose(2, 0, 1, 3)
    qkv_b_grad = spread_core(qkv_b_grad, 3, inner * wide)
    small_grads = [
        total_of(norm1_grad * normal),
        total_of(norm1_grad),
        total_of(norm2_grad * normal),
        total_of(norm2_grad),
        qkv_b_grad,
        shift_grad,
        spread_core(up_b_grad, 1, ff // dp),
    ]
    small_sizes = [value.shape[0] // devices for value in small_grads]
    total = jnp.concatenate([value.reshape(devices, -1) for value in small_grads], axis=1)
    total = jnp.pad(total, ((0, 0), (0, -total.shape[1] % 128)))
    total = total.reshape((2,) * (len(bits) + 1) + (1, -1))

    last = [
        Reduction(sent_a, dot(kept_a, rest_a[1], TN), xyz, True),
        Reduction(sent_b, dot(kept_b, rest_b[1], TN), yxz, True),
        dense,
    ]
    names = names_of(True)
    for at, (axis, bit) in enumerate(xyz + [("dp", 1)]):
        dim = names.index((axis, bit))
        names.pop(dim)
        if last[0].order:
            held = [one.total for one in last]
            held, total = lax.optimization_barrier((held, total))
            if at == 0:
                sides = after((branch[half_rows:], slope[half_rows:]), held)
                came = [swap(value, "dp", 1) for value in sides]
            if len(last[0].order) == 1:
                output, input_grad = finish(branch, slope, *after(came, held))
            for one, value in zip(last, held):
                one.total = value
                if one.order:
                    one.step()
        total = reduce_stage(total, dim, axis, bit, F32)
    qkv_a, qkv_b, dense_w_grad = [one.result() for one in last]
    down_w_grad, up_w_grad = [one.result() for one in feed]
    up_w_grad = columns_home(up_w_grad, 1)
    qkv_w_grad = columns_home(jnp.concatenate([qkv_a, qkv_b], axis=-1), 3)
    total = total.reshape(-1)
    smalls, at = [], 0
    for size in small_sizes:
        smalls.append(total[at : at + size])
        at += size
    return (
        output,
        input_grad,
        smalls[0],
        smalls[1],
        smalls[2],
        smalls[3],
        qkv_w_grad,
        smalls[4],
        dense_w_grad,
        smalls[5],
        up_w_grad,
        smalls[6],
        down_w_grad,
        smalls[5],
    )


def solution(mesh):
    rows = ("dp", "blk", "ulysses")
    tokens = P("dp", ("blk", "ulysses"), None)
    vector, matrix = P(rows), P(rows, None)
    in_specs = (tokens, P("dp", "blk")) + (vector,) * 4 + (matrix, vector) * 4 + (tokens,)
    out_specs = (tokens, tokens) + (vector,) * 4 + (matrix, vector) * 4
    return jax.shard_map(
        on_device, mesh=mesh, in_specs=in_specs, out_specs=out_specs, check_vma=False
    )
```

```python
from functools import partial

import jax
import jax.numpy as jnp
from jax import lax
from jax.experimental import pallas as pl
from jax.experimental.pallas import tpu as pltpu
from jax.sharding import PartitionSpec as P

HEADS = 16
HEAD_DIM = 64
ROT = 16
EPSILON = 1e-05
MASKED_SCORE = -1e30
LOG2_E = 1.4426950408889634
RANKS = ("blk", "ulysses")
F32 = jnp.float32
BF16 = jnp.bfloat16
NN = (((1,), (0,)), ((), ()))
NT = (((1,), (1,)), ((), ()))
TN = (((0,), (0,)), ((), ()))
ANY = pl.BlockSpec(memory_space=pl.ANY)
VMEM = pl.BlockSpec(memory_space=pltpu.VMEM)
SMEM = pl.BlockSpec(memory_space=pltpu.SMEM)


def dot(left, right, dims=NN):
    return lax.dot_general(left, right, dims, preferred_element_type=F32)


def swap(value, axis, bit):
    size = lax.axis_size(axis)
    return lax.ppermute(value, axis, [(i, i ^ bit) for i in range(size)])


def bits_of(size):
    return [1 << k for k in range(size.bit_length() - 1)]


def gather(value, stages):
    for axis, bit in stages:
        value = jnp.concatenate([value, swap(value, axis, bit)], axis=0)
    return value


def after(value, other):
    return lax.optimization_barrier((value, other))[0]


def gather_pair(value, stages):
    value = gather(value, stages[:-1])
    return [value, swap(value, *stages[-1])]


def natural_weight(axis, bit):
    ulysses = lax.axis_size("ulysses")
    if axis == "ulysses":
        return bit
    if axis == "blk":
        return bit * ulysses
    return (bit // 2) * ulysses * lax.axis_size("blk")


def places_of(stages, mine):
    slot = jnp.arange(1 << len(stages), dtype=jnp.int32)
    relative = jnp.zeros_like(slot)
    for at, (axis, bit) in enumerate(stages):
        relative = relative + ((slot >> at) % 2) * natural_weight(axis, bit)
    return relative ^ mine


def own_bit(axis, bit):
    return (lax.axis_index(axis) // bit) % 2


def pick(value, index, dim):
    return lax.dynamic_index_in_dim(value, index, dim, keepdims=False)


def reduce_stage(total, dim, axis, bit, wire=BF16):
    mine = own_bit(axis, bit)
    sent = pick(total, 1 - mine, dim).astype(wire)
    return pick(total, mine, dim) + swap(sent, axis, bit).astype(F32)


def params(mib):
    return pltpu.CompilerParams(vmem_limit_bytes=mib << 20)


class Sems:
    def __init__(self, array):
        self.array, self.used = array, 0

    def copy(self, source, target):
        self.used += 1
        return pltpu.make_async_copy(source, target, self.array.at[self.used - 1])


def run(copies):
    for copy in copies:
        copy.start()
    for copy in copies:
        copy.wait()


def slot_refs(refs):
    return [ref.at[at] for ref in refs for at in range(ref.shape[0])]


def in_order(buffers, places, direct):
    if direct:
        return buffers, places
    natural = jnp.arange(places.shape[0], dtype=jnp.int32)
    whole = jnp.concatenate(buffers, axis=0)
    return [jnp.take(whole, jnp.argsort(places), axis=0)], natural


def rotate(value, cosine, sine, sign):
    lane = lax.broadcasted_iota(jnp.int32, value.shape, 1) % HEAD_DIM
    lanes = value.shape[1]
    other = jnp.where(
        lane < ROT // 2,
        pltpu.roll(value, lanes - ROT // 2, 1),
        pltpu.roll(value, ROT // 2, 1),
    )
    return value * cosine + other * (sine * sign)


def first_kernel(plan, places, counts, place_a, place_b, *rest):
    ranks, seqs, per_rank, tokens, wide = plan
    planes, inner, piece = places
    x_ref, cot_ref, bias_ref, cos_ref, sin_ref = rest[:5]
    a_refs, b_refs = rest[5 : 5 + counts[0]], rest[5 + counts[0] : 5 + sum(counts)]
    rest = rest[5 + sum(counts) :]
    out_refs, (w_ref, dense_ref, in_sems) = rest[:per_rank], rest[per_rank:]
    seq_groups = seqs // per_rank
    groups = ranks // seq_groups
    width = x_ref.shape[1]
    half = width // 2
    give = Sems(in_sems)
    copies = []
    for slots, place_ref, second in ((a_refs, place_a, False), (b_refs, place_b, True)):
        for at, slot in enumerate(slot_refs(slots)):
            place = place_ref[at]
            for part in range(2):
                source = slot.at[pl.ds(part * piece, piece)]
                row = ((place // inner) * 2 + part) * inner + place % inner
                span = pl.ds(pl.multiple_of(row * piece, piece), piece)
                if second:
                    own = pl.ds(pl.multiple_of(place * piece, piece), piece)
                    copies.append(
                        give.copy(source.at[:, pl.ds(0, half)], w_ref.at[span, pl.ds(width, half)])
                    )
                    copies.append(
                        give.copy(
                            source.at[:, pl.ds(half, half)],
                            dense_ref.at[own, pl.ds(part * half, half)],
                        )
                    )
                else:
                    copies.append(give.copy(source, w_ref.at[span, pl.ds(0, width)]))
    run(copies)

    for q in range(per_rank):
        held = out_refs[q]

        def step(group, carry):
            rows = pl.ds(pl.multiple_of((group * per_rank + q) * tokens, tokens), tokens)
            x = x_ref[rows, :]
            cosine, sine = cos_ref[rows, :], sin_ref[rows, :]
            grads = dot(cot_ref[rows, :], dense_ref[...], NT).astype(BF16)
            for g in range(groups):
                cols = slice(3 * g * wide, 3 * (g + 1) * wide)
                joined = dot(x, w_ref[:, cols]) + bias_ref[:, cols]
                turned = rotate(joined[:, : 2 * wide], cosine, sine, 1.0)
                rank = g * seq_groups + group
                held[rank, :, : 2 * wide] = turned.astype(BF16)
                held[rank, :, 2 * wide : 3 * wide] = joined[:, 2 * wide :].astype(BF16)
                held[rank, :, 3 * wide :] = grads[:, g * wide : (g + 1) * wide]
            return carry

        lax.fori_loop(0, seq_groups, step, 0)


def first_chunks(plan, places, a, b, place_a, place_b, x, cot, bias, cosine, sine):
    ranks, seqs, per_rank, tokens, wide = plan
    width = x.shape[1]
    slots = place_a.shape[0]
    outs = pl.pallas_call(
        partial(first_kernel, plan, places, (len(a), len(b))),
        in_specs=[SMEM] * 2 + [VMEM] * 5 + [ANY] * (len(a) + len(b)),
        out_specs=[VMEM] * (per_rank + 2),
        out_shape=[jax.ShapeDtypeStruct((ranks, tokens, 4 * wide), BF16)] * per_rank
        + [
            jax.ShapeDtypeStruct((width, 3 * width // 2), BF16),
            jax.ShapeDtypeStruct((width // 2, width), BF16),
        ],
        scratch_shapes=[pltpu.SemaphoreType.DMA((6 * slots,))],
        compiler_params=params(48),
        cost_estimate=pl.CostEstimate(
            flops=4 * x.shape[0] * width * width, bytes_accessed=20 << 20, transcendentals=0
        ),
        name="first_chunks",
    )(place_a, place_b, x, cot, bias, cosine, sine, *a, *b)
    return outs[:per_rank], outs[per_rank], outs[per_rank + 1]


def feed_kernel(places, counts, block, side_unit, up_place, down_place, half_ref, x_ref, cot_ref, bias_ref, *rest):
    planes, inner, piece = places
    up_refs, down_refs = rest[: counts[0]], rest[counts[0] : sum(counts)]
    rest = rest[sum(counts) :]
    up_send, up_keep, down_send, down_keep, out_ref, norm_ref, sum_ref = rest[:7]
    up_w, down_w, act, grad, up_s, up_k, down_s, down_k, in_sems, sems = rest[7:]
    rows, width = x_ref.shape
    ff = down_w.shape[0]
    blocks = ff // block
    tile = rows // 2
    give = Sems(in_sems)
    copies = []
    for at, slot in enumerate(slot_refs(up_refs)):
        place = up_place[at]
        for part in range(2):
            row = ((place // inner) * 2 + part) * inner + place % inner
            span = pl.ds(pl.multiple_of(row * piece, piece), piece)
            copies.append(give.copy(slot.at[pl.ds(part * piece, piece)], up_w.at[span]))
    unit = down_refs[0].shape[1]
    for at, slot in enumerate(slot_refs(down_refs)):
        span = pl.ds(pl.multiple_of(down_place[at] * unit, unit), unit)
        copies.append(give.copy(slot, down_w.at[span]))
    run(copies)
    mine, mine_block = half_ref[0], half_ref[1]
    span_half = pl.ds(pl.multiple_of(mine * (width // 2), width // 2), width // 2)
    span_other = pl.ds(pl.multiple_of((1 - mine) * (width // 2), width // 2), width // 2)

    def out_copies(step):
        cols = pl.ds(pl.multiple_of(natural(step) * block, block), block)
        at = step % (blocks // 2)
        span = pl.ds(pl.multiple_of(at * block, block), block)
        return [
            pltpu.make_async_copy(up_s.at[step], up_send.at[:, cols], sems.at[0, step]),
            pltpu.make_async_copy(up_k.at[step], up_keep.at[:, cols], sems.at[1, step]),
        ], span

    def natural(step):
        side = jnp.where(step < blocks // 2, 1 - mine_block, mine_block)
        at = step % (blocks // 2)
        return ((at // side_unit) * 2 + side) * side_unit + at % side_unit

    def one(step, carry):
        at = natural(step)
        cols = pl.ds(pl.multiple_of(at * block, block), block)
        up_b = up_w[:, cols]
        down_b = down_w[cols, :]
        bias = bias_ref[:, cols]
        for r in range(2):
            span = slice(r * tile, (r + 1) * tile)
            pre = dot(x_ref[span, :], up_b) + bias
            cdf = 0.5 * (1.0 + lax.erf(pre * (0.5**0.5)))
            slope = cdf + pre * (jnp.exp2(pre * pre * (-0.5 * LOG2_E)) * 0.3989422804014327)
            active = (pre * cdf).astype(BF16)
            act[span, :] = active
            back = (dot(cot_ref[span, :], down_b, NT) * slope).astype(BF16)
            grad[span, :] = back
            out = dot(active, down_b)
            norm = dot(back, up_b, NT)

            @pl.when(step == 0)
            def _():
                out_ref[span, :] = out
                norm_ref[span, :] = norm

            @pl.when(step > 0)
            def _():
                out_ref[span, :] += out
                norm_ref[span, :] += norm

        sum_ref[:, cols] = jnp.sum(grad[...].astype(F32), axis=0, keepdims=True)
        up_g = dot(x_ref[:, span_other], grad[...], TN)
        up_s[step] = up_g.astype(BF16)
        up_k[step] = dot(x_ref[:, span_half], grad[...], TN)
        pair, span = out_copies(step)
        for copy in pair:
            copy.start()
        down_g = dot(act[...], cot_ref[...], TN)

        @pl.when(step < blocks // 2)
        def _():
            down_s[step] = down_g.astype(BF16)
            pltpu.make_async_copy(down_s.at[step], down_send.at[span], sems.at[2, step]).start()

        @pl.when(step >= blocks // 2)
        def _():
            here = step - blocks // 2
            down_k[here] = down_g
            pltpu.make_async_copy(down_k.at[here], down_keep.at[span], sems.at[2, step]).start()

        return carry

    lax.fori_loop(0, blocks, one, 0)
    for step in range(blocks):
        pair, span = out_copies(step)
        for copy in pair:
            copy.wait()
        if step < blocks // 2:
            pltpu.make_async_copy(down_s.at[step], down_send.at[span], sems.at[2, step]).wait()
        else:
            here = step - blocks // 2
            pltpu.make_async_copy(down_k.at[here], down_keep.at[span], sems.at[2, step]).wait()


def feed_forward(places, half, x, cot, bias, up, up_place, down, down_place):
    rows, width = x.shape
    ff = bias.shape[1]
    block = min(256, ff // 2)
    blocks = ff // block
    return pl.pallas_call(
        partial(feed_kernel, places, (len(up), len(down)), block, blocks // (2 * places[0])),
        in_specs=[SMEM] * 3 + [VMEM] * 3 + [ANY] * (len(up) + len(down)),
        out_specs=[ANY] * 4 + [VMEM] * 3,
        out_shape=[
            jax.ShapeDtypeStruct((width // 2, ff), BF16),
            jax.ShapeDtypeStruct((width // 2, ff), F32),
            jax.ShapeDtypeStruct((ff // 2, width), BF16),
            jax.ShapeDtypeStruct((ff // 2, width), F32),
            jax.ShapeDtypeStruct((rows, width), F32),
            jax.ShapeDtypeStruct((rows, width), F32),
            jax.ShapeDtypeStruct((1, ff), F32),
        ],
        scratch_shapes=[
            pltpu.VMEM((width, ff), BF16),
            pltpu.VMEM((ff, width), BF16),
            pltpu.VMEM((rows, block), BF16),
            pltpu.VMEM((rows, block), BF16),
            pltpu.VMEM((blocks, width // 2, block), BF16),
            pltpu.VMEM((blocks, width // 2, block), F32),
            pltpu.VMEM((blocks // 2, block, width), BF16),
            pltpu.VMEM((blocks // 2, block, width), F32),
            pltpu.SemaphoreType.DMA((2 * up_place.shape[0] + down_place.shape[0],)),
            pltpu.SemaphoreType.DMA((3, blocks)),
        ],
        compiler_params=params(58),
        cost_estimate=pl.CostEstimate(
            flops=12 * rows * width * ff, bytes_accessed=32 << 20, transcendentals=2 * rows * ff
        ),
        name="feed_forward",
    )(up_place, down_place, half, x, cot, bias, *up, *down)


def attention_kernel(low_ref, start_ref, chunk, *rest):
    outs, turned, natural, scores, products, sums = rest
    ranks, block, wide = chunk.shape[0], chunk.shape[1], chunk.shape[2] // 4
    heads = wide // HEAD_DIM
    scale = HEAD_DIM ** (-0.5)
    power = scale * LOG2_E
    def prepare(b, carry):
        kinds = chunk[b]
        turned[b] = kinds.T
        for h in range(heads):
            own = slice(h * HEAD_DIM, (h + 1) * HEAD_DIM)
            for kind in range(4):
                natural[h, kind, b] = kinds[:, kind * wide : (kind + 1) * wide][:, own]
            sums[h, 0, b] = jnp.zeros((block, HEAD_DIM), F32)
            sums[h, 1, b] = jnp.zeros((block, HEAD_DIM), F32)
        return carry

    lax.fori_loop(0, ranks, prepare, 0)

    def rows_of(h, kind):
        return slice(kind * wide + h * HEAD_DIM, kind * wide + (h + 1) * HEAD_DIM)

    def queries(i, carry):
        start = start_ref[i]
        query = i * block + lax.broadcasted_iota(jnp.int32, (1, block), 1)
        low = low_ref[i]

        first, last = low // 2, (i + 2) // 2

        def score(pair, tops):
            for j in (2 * pair, 2 * pair + 1):
                key = j * block + lax.broadcasted_iota(jnp.int32, (block, block), 0)
                allowed = (key <= query) & (key >= start)
                found = []
                for h in range(heads):
                    value = dot(natural[h, 1, j], turned[i, rows_of(h, 0), :])
                    value = jnp.where(allowed, value, MASKED_SCORE)
                    scores[h, j] = value
                    found.append(jnp.maximum(tops[h], jnp.max(value, axis=0, keepdims=True)))
                tops = tuple(found)
            return tops

        tops = lax.fori_loop(first, last, score, (jnp.full((1, block), MASKED_SCORE, F32),) * heads)

        def weigh(pair, carried):
            for j in (2 * pair, 2 * pair + 1):
                found = []
                for h in range(heads):
                    total, delta = carried[h]
                    expo = jnp.exp2((scores[h, j] - tops[h]) * power)
                    scores[h, j] = expo
                    product = dot(natural[h, 2, j], turned[i, rows_of(h, 3), :])
                    products[h, j] = product
                    found.append(
                        (
                            total + jnp.sum(expo, axis=0, keepdims=True),
                            delta + jnp.sum(expo * product, axis=0, keepdims=True),
                        )
                    )
                carried = tuple(found)
            return carried

        zero = jnp.zeros((1, block), F32)
        stats = lax.fori_loop(first, last, weigh, ((zero, zero),) * heads)
        inverse = [1.0 / total for total, _ in stats]
        deltas = [delta * inv for (_, delta), inv in zip(stats, inverse)]

        def collect(pair, carried):
            for j in (2 * pair, 2 * pair + 1):
                found = []
                for h in range(heads):
                    mixed, query_grad = carried[h]
                    prob = scores[h, j] * inverse[h]
                    rounded = prob.astype(BF16)
                    slope = (prob * (products[h, j] - deltas[h])).astype(BF16)
                    mixed = mixed + dot(turned[j, rows_of(h, 2), :], rounded)
                    query_grad = query_grad + dot(turned[j, rows_of(h, 1), :], slope)
                    sums[h, 0, j] += dot(slope, natural[h, 0, i])
                    sums[h, 1, j] += dot(rounded, natural[h, 3, i])
                    found.append((mixed, query_grad))
                carried = tuple(found)
            return carried

        empty = jnp.zeros((HEAD_DIM, block), F32)
        totals = lax.fori_loop(first, last, collect, ((empty, empty),) * heads)
        mixed = jnp.concatenate([t[0] for t in totals], axis=0)
        query_grad = jnp.concatenate([t[1] for t in totals], axis=0)
        outs[i, :, :wide] = mixed.T.astype(BF16)
        outs[i, :, wide : 2 * wide] = (query_grad * scale).T.astype(BF16)
        return carry

    lax.fori_loop(0, ranks, queries, 0)

    def finish(b, carry):
        for kind in range(2):
            value = jnp.concatenate([sums[h, kind, b] for h in range(heads)], axis=1)
            if kind == 0:
                value = value * scale
            outs[b, :, (2 + kind) * wide : (3 + kind) * wide] = value.astype(BF16)
        return carry

    lax.fori_loop(0, ranks, finish, 0)


def attention(low, start, chunk):
    ranks, block, wide = chunk.shape[0], chunk.shape[1], chunk.shape[2] // 4
    heads = wide // HEAD_DIM
    pairs = ranks * (ranks + 1) // 2 * block * block * heads
    return pl.pallas_call(
        attention_kernel,
        in_specs=[SMEM, VMEM, VMEM],
        out_specs=VMEM,
        out_shape=jax.ShapeDtypeStruct(chunk.shape, BF16),
        scratch_shapes=[
            pltpu.VMEM((ranks, 4 * wide, block), BF16),
            pltpu.VMEM((heads, 4, ranks, block, HEAD_DIM), BF16),
            pltpu.VMEM((heads, ranks, block, block), F32),
            pltpu.VMEM((heads, ranks, block, block), F32),
            pltpu.VMEM((heads, 2, ranks, block, HEAD_DIM), F32),
        ],
        compiler_params=params(56),
        cost_estimate=pl.CostEstimate(
            flops=2 * 6 * 4 * HEAD_DIM * pairs,
            bytes_accessed=8 * ranks * block * wide * 2,
            transcendentals=pairs,
        ),
        name="attention",
    )(low, start, chunk)


def return_kernel(plan, cos_ref, sin_ref, *rest):
    ranks, seqs, per_rank, tokens, wide = plan
    in_refs, (mixed_ref, grad_ref) = rest[:per_rank], rest[per_rank:]
    seq_groups = seqs // per_rank
    groups = ranks // seq_groups
    for q in range(per_rank):
        held = in_refs[q]

        def step(group, carry):
            rows = pl.ds(pl.multiple_of((group * per_rank + q) * tokens, tokens), tokens)
            cosine, sine = cos_ref[rows, :], sin_ref[rows, :]
            for g in range(groups):
                value = held[g * seq_groups + group]
                mixed_ref[rows, g * wide : (g + 1) * wide] = value[:, :wide]
                turned = rotate(value[:, wide : 3 * wide].astype(F32), cosine, sine, -1.0)
                at = 3 * g * wide
                grad_ref[rows, at : at + 2 * wide] = turned.astype(BF16)
                grad_ref[rows, at + 2 * wide : at + 3 * wide] = value[:, 3 * wide :]
            return carry

        lax.fori_loop(0, seq_groups, step, 0)


def return_chunks(plan, cosine, sine, chunks):
    ranks, seqs, per_rank, tokens, wide = plan
    groups = ranks * per_rank // seqs
    return pl.pallas_call(
        partial(return_kernel, plan),
        in_specs=[VMEM] * (2 + per_rank),
        out_specs=[VMEM, VMEM],
        out_shape=[
            jax.ShapeDtypeStruct((seqs * tokens, groups * wide), BF16),
            jax.ShapeDtypeStruct((seqs * tokens, 3 * groups * wide), BF16),
        ],
        compiler_params=params(40),
        cost_estimate=pl.CostEstimate(
            flops=8 * seqs * tokens * 4 * groups * wide, bytes_accessed=12 << 20, transcendentals=0
        ),
        name="return_chunks",
    )(cosine, sine, *chunks)


def on_device(
    hidden,
    positions,
    ln1_gain,
    ln1_bias,
    ln2_gain,
    ln2_bias,
    qkv_weight,
    qkv_bias,
    dense_weight,
    dense_bias,
    up_weight,
    up_bias,
    down_weight,
    down_bias,
    cotangent,
):
    seq_dp, tokens, width = hidden.shape
    ulysses, blk, dp = lax.axis_size("ulysses"), lax.axis_size("blk"), lax.axis_size("dp")
    planes = dp // 2
    ranks = blk * ulysses
    core = lax.axis_index("dp") % 2
    rank = lax.axis_index("blk") * ulysses + lax.axis_index("ulysses")
    mine = (lax.axis_index("dp") // 2) * ranks + rank
    devices = dp * ranks
    half_rows = seq_dp * tokens
    rows = 2 * half_rows
    piece = width // devices
    ff = up_weight.shape[1]

    seqs = 2 * seq_dp
    pairs = seqs * (HEADS // 2) // ranks
    heads_each = 2 if pairs % 2 == 0 else 1
    seqs_each = pairs // heads_each
    seq_groups = seqs // seqs_each
    groups = HEADS // 2 // heads_each
    wide = heads_each * HEAD_DIM

    def with_partner(value):
        return jnp.concatenate([value, swap(value, "dp", 1)], axis=0)

    stage_z = [("ulysses", bit) for bit in reversed(bits_of(ulysses))]
    stage_y = [("blk", bit) for bit in bits_of(blk)]
    stage_x = [("dp", bit) for bit in bits_of(dp)[1:]]
    order_a, order_b = stage_z + stage_y + stage_x, stage_z + stage_x + stage_y

    def core_columns(value, lead, index):
        value = value.reshape(lead, 3, planes, 2, HEADS // dp // heads_each, wide)
        value = pick(value, index, 3)
        return value.transpose(0, 2, 3, 1, 4).reshape(lead, 3 * width // 2)

    def core_ff(value, lead, index):
        return pick(value.reshape(lead, planes, 2, ff // dp), index, 2).reshape(lead, ff // 2)

    def both_cores(kept, sent):
        came = swap(sent, "dp", 1)
        return jnp.concatenate(
            [jnp.where(core == 0, kept, came), jnp.where(core == 0, came, kept)], axis=0
        )

    qkv_piece = both_cores(
        core_columns(qkv_weight, piece, core), core_columns(qkv_weight, piece, 1 - core)
    )
    dense_piece = jnp.concatenate(
        [dense_weight[:, : width // 2], dense_weight[:, width // 2 :]], axis=0
    )
    first = jnp.concatenate([qkv_piece, dense_piece], axis=1)[None]
    small = [ln1_gain, ln1_bias, ln2_gain, ln2_bias, qkv_bias, dense_bias, up_bias, down_bias]
    sizes = [value.shape[0] for value in small]
    length = sum(sizes)
    padded = -(-length // 128) * 128
    packed = jnp.concatenate(small + [jnp.zeros((padded - length,), BF16)])[None]
    places = with_partner(positions)
    every = gather(places[None], stage_y)
    up_piece = both_cores(core_ff(up_weight, piece, core), core_ff(up_weight, piece, 1 - core))
    up_part, down_part = up_piece[None], down_weight[None]

    packed = gather(packed, [("dp", 1)])
    beside = stage_x + stage_y
    for at, stage in enumerate(stage_z):
        packed = gather(after(packed, (first, every)), beside[at : at + 1])
        first = gather(first, [stage])
        if at == 0:
            up_part, down_part = after((up_part, down_part), first)
    up_part, down_part = gather(up_part, stage_z[:1]), gather(down_part, stage_z[:1])
    packed = gather(after(packed, first), beside[len(stage_z) :] + stage_z[:1])

    direct = piece % 16 == 0
    units = (planes, ranks, piece)
    places_a, places_b = places_of(order_a, mine), places_of(order_b, mine)
    first_a = gather_pair(first[..., :width], stage_y + stage_x)
    first_b = gather_pair(first[..., width:], stage_x + stage_y)
    packed = gather(after(packed, (first_a[0], first_b[0])), stage_z[1:])
    up_part, down_part = after((up_part, down_part), (packed, first_a[0], first_b[0]))
    up_part, down_part = gather(up_part, stage_z[1:]), gather(down_part, stage_z[1:])
    early = (up_part, down_part)
    first_a, place_a = in_order(first_a, places_a, direct)
    first_b, place_b = in_order(first_b, places_b, direct)

    relative = jnp.zeros((devices,), jnp.int32)
    weights = [ranks] + [
        natural_weight(axis, bit) * (2 if axis == "dp" else 1)
        for axis, bit in beside + stage_z
    ]
    for at, weight in enumerate(weights):
        relative = relative + ((jnp.arange(devices, dtype=jnp.int32) >> at) % 2) * weight
    home = (lax.axis_index("dp") * ranks + rank) ^ relative
    sorting = (jnp.arange(devices, dtype=jnp.int32)[:, None] == home[None, :]).astype(BF16)
    packed = dot(sorting, packed)
    vectors, at = [], 0
    for size in sizes:
        vectors.append(packed[:, at : at + size].reshape(-1))
        at += size
    gain_one, bias_one, gain_two, bias_two, qkv_shift, dense_shift, up_shift, down_shift = vectors
    qkv_shift = core_columns(qkv_shift, 1, core)
    up_shift = core_ff(up_shift, 1, core)

    inputs = with_partner(hidden.reshape(half_rows, width))
    upstream = with_partner(cotangent.reshape(half_rows, width))
    wide_inputs = inputs.astype(F32)
    center = wide_inputs - jnp.mean(wide_inputs, axis=-1, keepdims=True)
    spread = lax.rsqrt(jnp.mean(center * center, axis=-1, keepdims=True) + EPSILON)
    normal = center * spread
    norm1 = (normal * gain_one + bias_one).astype(BF16)
    norm2 = (normal * gain_two + bias_two).astype(BF16)

    own_places = lax.dynamic_slice_in_dim(
        places, lax.axis_index("ulysses") * tokens, tokens, 1
    ).reshape(rows, 1)
    lane = jnp.arange(2 * wide, dtype=jnp.int32) % HEAD_DIM
    freqs = 10000.0 ** (-((lane % (ROT // 2)).astype(F32) * 2.0 / ROT))
    freqs = jnp.where(lane < ROT, freqs, 0.0)
    angles = own_places.astype(F32) * freqs
    cosine = jnp.cos(angles)
    sine = jnp.sin(angles) * jnp.where(lane < ROT // 2, -1.0, 1.0)

    here = lax.axis_index("blk")
    every = jnp.stack([pick(every, here ^ j, 0) for j in range(blk)], axis=1)
    every = every.reshape(seqs, ranks * tokens)
    starts = jnp.arange(ranks * tokens, dtype=jnp.int32) - every
    starts = pick(starts.reshape(seq_groups, seqs_each, ranks, 1, tokens), rank % seq_groups, 0)
    lows = starts[:, :, 0, 0] // tokens

    def exchange(chunks):
        return lax.all_to_all(chunks, RANKS, split_axis=0, concat_axis=0, tiled=True)

    plan = (ranks, seqs, seqs_each, tokens, wide)
    sent, qkv_full, dense_full = first_chunks(
        plan, units, first_a, first_b, place_a, place_b,
        after(norm1, early), upstream, qkv_shift, cosine, sine,
    )
    up_part, down_part = gather(up_part, stage_y[:1]), gather(down_part, stage_x[:1])
    chunks = [exchange(sent[0])]
    chunks += [exchange(after(value, (chunks[0], up_part, down_part))) for value in sent[1:]]
    solved = [attention(lows[0], starts[0], chunks[0])]

    up_bufs, up_place = in_order(gather_pair(up_part, stage_y[1:] + stage_x), places_a, direct)
    down_bufs, down_place = in_order(
        gather_pair(down_part, stage_x[1:] + stage_y), places_b, direct
    )
    half = jnp.stack([own_bit(*stage_x[-1]), own_bit(*stage_y[-1])]).astype(jnp.int32)
    up_send, up_keep, down_send, down_keep, mlp, norm2_grad, up_b_grad = feed_forward(
        units, half, after(norm2, (solved[0], chunks)), upstream, up_shift,
        up_bufs, up_place, down_bufs, down_place,
    )
    returned = [exchange(solved[0])]
    up_send, up_keep, down_send, down_keep = after(
        (up_send, up_keep, down_send, down_keep), returned[0]
    )
    part = returned[0]
    for q in range(1, seqs_each):
        chunk = after(chunks[q], (up_b_grad, returned[-1]))
        solved.append(attention(lows[q], starts[q], chunk))
        part = exchange(solved[q][:, : tokens // 4])
        rest = exchange(after(solved[q][:, tokens // 4 :], part))
        returned.append(jnp.concatenate([part, rest], axis=1))

    def halves(left, axis, bit, names):
        dim = names.index((axis, bit))
        span = left.shape[1] >> (dim + 1)
        mine_bit = own_bit(axis, bit)
        return [
            jnp.concatenate(
                [
                    lax.dynamic_slice_in_dim(left, 2 * at * span + index * span, span, 1)
                    for at in range(1 << dim)
                ],
                axis=1,
            )
            for index in (1 - mine_bit, mine_bit)
        ]

    bits = [("dp", bit) for bit in reversed(bits_of(dp)[1:])]
    bits += [("blk", bit) for bit in reversed(bits_of(blk))]
    bits += [("ulysses", bit) for bit in reversed(bits_of(ulysses))]
    low_z = list(reversed(stage_z))

    def names_of(with_core):
        return bits[: len(stage_x)] + [("dp", 1)] * with_core + bits[len(stage_x) :]

    class Reduction:
        def __init__(self, sent, total, order, with_core):
            self.names = names_of(with_core)
            self.order, self.with_core = order, with_core
            if sent is not None:
                self.names.remove(order[0])
                self.order = order[1:]
                total = total + swap(sent, *order[0]).astype(F32)
            units = total.shape[0] >> len(self.names)
            self.total = total.reshape((2,) * len(self.names) + (units, total.shape[1]))

        def pop(self):
            axis, bit = self.order[0]
            dim = self.names.index((axis, bit))
            self.names.pop(dim)
            self.order = self.order[1:]
            return dim, axis, bit

        def step(self):
            dim, axis, bit = self.pop()
            self.total = reduce_stage(self.total, dim, axis, bit)

        def result(self):
            if self.with_core:
                return jnp.where(core == 0, self.total, self.total[::-1])
            return self.total

    def step_together(reductions):
        sent, kept = [], []
        for one in reductions:
            dim, axis, bit = one.pop()
            mine_bit = own_bit(axis, bit)
            part = pick(one.total, 1 - mine_bit, dim).astype(BF16)
            cols = part.reshape(-1, part.shape[-1])
            sent += [cols[:, at : at + width] for at in range(0, cols.shape[1], width)]
            kept.append(pick(one.total, mine_bit, dim))
        came = swap(jnp.concatenate(sent, axis=0), axis, bit).astype(F32)
        at = 0
        for one, keep in zip(reductions, kept):
            count = keep.shape[-1] // width
            rows_each = keep.size // keep.shape[-1]
            cols = [came[at + k * rows_each : at + (k + 1) * rows_each] for k in range(count)]
            at += count * rows_each
            one.total = keep + jnp.concatenate(cols, axis=1).reshape(keep.shape)

    def products(left, right, order, with_core):
        sent, kept = halves(left, *order[0], names_of(with_core))
        return dot(sent, right, TN).astype(BF16), kept, right

    xyz, yxz = stage_x[::-1] + stage_y[::-1] + low_z, stage_y[::-1] + stage_x[::-1] + low_z
    feed = [
        Reduction(down_send, down_keep, yxz, False),
        Reduction(up_send, up_keep, xyz, True),
    ]
    while len(feed[0].order) > len(low_z):
        for one in feed:
            one.total = after(one.total, part)
            one.step()
    for one, value in zip(feed, after([one.total for one in feed], returned[-1])):
        one.total = value
    while len(feed[0].order) > 1:
        step_together(feed)
    mixed, joined_grad = return_chunks(plan, cosine, sine, returned)
    cut = joined_grad.shape[1] // 2
    sent_a, *rest_a = products(norm1, joined_grad[:, :cut], xyz, True)
    sent_b, *rest_b = products(norm1, joined_grad[:, cut:], yxz, True)
    dense = Reduction(None, dot(mixed, upstream, TN), low_z + stage_x + stage_y, False)
    later = (sent_a, sent_b, dense.total)
    dense.step()
    grads_later, mixed_later, kept_a, kept_b = after(
        (joined_grad, mixed, rest_a[0], rest_b[0]), later
    )
    norm1_grad = dot(grads_later, qkv_full, NT)

    def columns_home(total, kinds):
        other = swap(total[1], "dp", 1)
        kept = total[0]
        pair = [jnp.where(core == 0, kept, other), jnp.where(core == 0, other, kept)]
        lead = kept.shape[0]
        if kinds == 1:
            pair = [value.reshape(lead, planes, ff // dp) for value in pair]
            return jnp.stack(pair, axis=2).reshape(lead, ff)
        inner = HEADS // dp // heads_each
        pair = [
            value.reshape(lead, planes, inner, 3, wide).transpose(0, 3, 1, 2, 4) for value in pair
        ]
        return jnp.stack(pair, axis=3).reshape(lead, 3 * width)

    branch = dot(mixed_later, dense_full) + mlp
    slope = norm1_grad * gain_one + norm2_grad * gain_two

    def finish(branch, slope, branch_came, slope_came):
        branch = branch[:half_rows] + branch_came
        output = wide_inputs[:half_rows] + (branch + dense_shift + down_shift)
        output = output.astype(BF16).reshape(hidden.shape)
        slope = slope[:half_rows] + slope_came
        own = normal[:half_rows]
        term = spread[:half_rows] * (
            slope
            - jnp.mean(slope, axis=-1, keepdims=True)
            - own * jnp.mean(slope * own, axis=-1, keepdims=True)
        )
        input_grad = upstream[:half_rows].astype(F32) + term
        return output, input_grad.astype(BF16).reshape(hidden.shape)

    def spread_core(value, kinds, last):
        value = value.reshape(kinds, planes, 1, last)
        empty = jnp.zeros_like(value)
        pair = [jnp.where(core == c, value, empty) for c in range(2)]
        return jnp.concatenate(pair, axis=2).reshape(-1)

    def total_of(value):
        return jnp.sum(value.astype(F32), axis=0)

    shift_grad = total_of(upstream[:half_rows])
    inner = HEADS // dp // heads_each
    qkv_b_grad = total_of(joined_grad).reshape(planes, inner, 3, wide).transpose(2, 0, 1, 3)
    qkv_b_grad = spread_core(qkv_b_grad, 3, inner * wide)
    small_grads = [
        total_of(norm1_grad * normal),
        total_of(norm1_grad),
        total_of(norm2_grad * normal),
        total_of(norm2_grad),
        qkv_b_grad,
        shift_grad,
        spread_core(up_b_grad, 1, ff // dp),
    ]
    small_sizes = [value.shape[0] // devices for value in small_grads]
    total = jnp.concatenate([value.reshape(devices, -1) for value in small_grads], axis=1)
    total = jnp.pad(total, ((0, 0), (0, -total.shape[1] % 128)))
    total = total.reshape((2,) * (len(bits) + 1) + (1, -1))

    last = [
        Reduction(sent_a, dot(kept_a, rest_a[1], TN), xyz, True),
        Reduction(sent_b, dot(kept_b, rest_b[1], TN), yxz, True),
        dense,
    ]
    names = names_of(True)
    for at, (axis, bit) in enumerate(xyz + [("dp", 1)]):
        dim = names.index((axis, bit))
        names.pop(dim)
        if last[0].order:
            held = [one.total for one in last]
            held, total = lax.optimization_barrier((held, total))
            if at == 0:
                sides = after((branch[half_rows:], slope[half_rows:]), held)
                came = [swap(value, "dp", 1) for value in sides]
            if len(last[0].order) == 1:
                output, input_grad = finish(branch, slope, *after(came, held))
                for one, value in zip(feed, after([one.total for one in feed], held)):
                    one.total = value
            for one, value in zip(last, held):
                one.total = value
                if one.order:
                    one.step()
            if not last[0].order:
                step_together(feed)
        total = reduce_stage(total, dim, axis, bit, F32)
    qkv_a, qkv_b, dense_w_grad = [one.result() for one in last]
    down_w_grad, up_w_grad = [one.result() for one in feed]
    up_w_grad = columns_home(up_w_grad, 1)
    qkv_w_grad = columns_home(jnp.concatenate([qkv_a, qkv_b], axis=-1), 3)
    total = total.reshape(-1)
    smalls, at = [], 0
    for size in small_sizes:
        smalls.append(total[at : at + size])
        at += size
    return (
        output,
        input_grad,
        smalls[0],
        smalls[1],
        smalls[2],
        smalls[3],
        qkv_w_grad,
        smalls[4],
        dense_w_grad,
        smalls[5],
        up_w_grad,
        smalls[6],
        down_w_grad,
        smalls[5],
    )


def solution(mesh):
    rows = ("dp", "blk", "ulysses")
    tokens = P("dp", ("blk", "ulysses"), None)
    vector, matrix = P(rows), P(rows, None)
    in_specs = (tokens, P("dp", "blk")) + (vector,) * 4 + (matrix, vector) * 4 + (tokens,)
    out_specs = (tokens, tokens) + (vector,) * 4 + (matrix, vector) * 4
    return jax.shard_map(
        on_device, mesh=mesh, in_specs=in_specs, out_specs=out_specs, check_vma=False
    )
```
